32 devices in a mesh: groups: 2 (over y), row: 4 (over z), col: 2 (over x), sub: 2 (over core).
Axes of the slice: x: 2, y: 2, z: 4, core: 2. Of those that a mesh axis runs over, the one named last changes fastest.
Arguments:
- pulses: bfloat16 [2, 8, 2, 256, 1024], P(None, ('groups', 'row'), None, 'sub'), parts along dimension 1, may hold values from -6 to 6
- owner: int32 [4], P('groups'), parts along dimension 0, may hold values from 0 to 3
- centres: int32 [8, 2, 2], P(('groups', 'row'), 'col'), parts along dimension 0, may hold values from 0 to 31
Outputs:
- formed_image: float32 [256, 2, 512], P(('groups', 'row'), None, ('col', 'sub')), parts along dimension 0
- despeckled: float32 [256, 512], P(('groups', 'row'), ('col', 'sub')), parts along dimension 0
The draws below stay inside these ranges and needn't reach their ends.
There are 2 independent parts, one for each index of `groups`. The reference program is written for one: setup_inputs(seed, part) draws one part's arguments, and reference() takes and returns one part's arrays. A program takes and returns all parts, laid end to end along the dimension named above; each array names one. Nothing has to cross between parts.
All inputs are finite; a program needn't handle non-finite values.
Results may differ from the reference program's by a relative error of at most 0.0068.
Values may be sent and summed in bfloat16 or wider, within the bound.
A program may use at most 64 MiB of HBM per device.

```python
import math
import jax
import jax.numpy as jnp
from jax import lax

F = 1024
PB = 256
NBLK = 2
TR = 32
TC = 128
RAD = 16
NR = 128
NC = 512
N_ROW = 4
N_COL = 2
N_SUB = 2


def set_ends(entries, own_key, low, largest):
    shape = entries.shape
    spot = [jax.random.randint(jax.random.fold_in(own_key, axis), (), 0, shape[axis]) for axis in range(len(shape))]
    entries = entries.at[tuple(spot)].set(low)
    longest = shape.index(max(shape))
    spot[longest] = (spot[longest] + 1) % shape[longest]
    return entries.at[tuple(spot)].set(largest)


def block_levels(own_key, shape, split, low, high):
    level = 1.0
    for dim, blocks in split:
        steps = jax.random.uniform(jax.random.fold_in(jax.random.fold_in(own_key, 6), dim), (blocks,), jnp.float32, low / len(split), high / len(split))
        level = level * jnp.repeat(jnp.exp(steps), shape[dim] // blocks).reshape((-1,) + (1,) * (len(shape) - 1 - dim))
    return level


def noise(rng, extent, scale, limit, shards=(), held_as=jnp.bfloat16):
    loudness = block_levels(rng, extent, shards, -0.22, 0.18) if shards else 1.0
    entries = jax.random.normal(rng, extent, jnp.float32) * scale * loudness
    return jnp.minimum(jnp.maximum(entries, -limit), limit).astype(held_as)


def setup_inputs(seed: int = 0, part: int = 0) -> dict:
    splits = jax.random.split(jax.random.key(seed), 4)
    own_keys = jax.random.split(jax.random.fold_in(splits[3], part), 4)
    return {
        "pulses": noise(own_keys[0], (NBLK, N_ROW, 2, PB, F), 1.0, 6.0, ((1, 4), (3, 2))),
        "owner": jax.random.randint(own_keys[1], (NBLK,), 0, N_ROW).astype(jnp.int32),
        "centres": set_ends(jax.random.randint(own_keys[2], (N_ROW, N_COL, 2), 0, TR), jax.random.fold_in(own_keys[2], 1), 0, TR - 1).astype(jnp.int32),
    }


SIGMA_RANGE = 1.0
TWO_PI = 2.0 * math.pi

def rephase(pulse_block, global_pulses, shift_rows, shift_cols, row_count):
    frequency = jnp.arange(F, dtype=jnp.int32)
    freq_index = frequency * shift_cols % F
    pulse_index = global_pulses * shift_rows % row_count
    phase_angle = TWO_PI * (freq_index.astype(jnp.float32)[None, :] / F + pulse_index.astype(jnp.float32)[:, None] / row_count)
    cosine = jnp.cos(phase_angle)
    sine_part = jnp.sin(phase_angle)
    real_part = pulse_block[0].astype(jnp.float32)
    imag_part = pulse_block[1].astype(jnp.float32)
    return ((real_part * cosine - imag_part * sine_part).astype(jnp.bfloat16), (real_part * sine_part + imag_part * cosine).astype(jnp.bfloat16))

def range_table(global_cols):
    frequency = jnp.arange(F, dtype=jnp.int32)
    phase_index = frequency[:, None] * global_cols[None, :] % F
    phase_angle = TWO_PI * phase_index.astype(jnp.float32) / F
    norm_scale = 1.0 / math.sqrt(F)
    return jnp.concatenate([(jnp.cos(phase_angle) * norm_scale).astype(jnp.bfloat16), (-jnp.sin(phase_angle) * norm_scale).astype(jnp.bfloat16)], axis=1)

def azimuth_table(global_rows, global_pulses, row_count):
    phase_index = global_rows[:, None] * global_pulses[None, :] % row_count
    phase_angle = TWO_PI * phase_index.astype(jnp.float32) / row_count
    norm_scale = 1.0 / math.sqrt(NBLK * PB)
    return jnp.concatenate([(jnp.cos(phase_angle) * norm_scale).astype(jnp.bfloat16), (-jnp.sin(phase_angle) * norm_scale).astype(jnp.bfloat16)], axis=1)

def compress(rephased_real, rephased_imag, freq_table):
    pulse_count = rephased_real.shape[0]
    col_count = freq_table.shape[1] // 2
    operand = jnp.concatenate([rephased_real, rephased_imag], axis=0)
    product = jnp.dot(operand, freq_table, preferred_element_type=jnp.float32)
    comp_real = (product[:pulse_count, :col_count] - product[pulse_count:, col_count:]).astype(jnp.bfloat16)
    comp_imag = (product[:pulse_count, col_count:] + product[pulse_count:, :col_count]).astype(jnp.bfloat16)
    return (comp_real, comp_imag)

def form_block(pulse_block, global_pulses, global_rows, freq_table, shift_rows, shift_cols, row_count):
    rephased_real, rephased_imag = rephase(pulse_block, global_pulses, shift_rows, shift_cols, row_count)
    comp_real, comp_imag = compress(rephased_real, rephased_imag, freq_table)
    az_table = azimuth_table(global_rows, global_pulses, row_count)
    stacked_rows = jnp.concatenate([jnp.concatenate([comp_real, comp_imag], axis=1), jnp.concatenate([-comp_imag, comp_real], axis=1)], axis=0)
    return jnp.dot(az_table, stacked_rows, preferred_element_type=jnp.float32)

def bilateral(padded, row_inside, col_inside):
    height = padded.shape[0] - 2 * RAD
    breadth = padded.shape[1] - 2 * RAD
    center = padded[RAD:RAD + height, RAD:RAD + breadth]
    numerator = center
    weight = jnp.ones_like(center)
    for distance in range(1, RAD + 1):
        spatial = 2.0 * distance * distance / (RAD * RAD)
        for offset in (-distance, distance):
            row_near = padded[RAD + offset:RAD + offset + height, RAD:RAD + breadth]
            row_flag = row_inside[RAD + offset:RAD + offset + height][:, None]
            col_near = padded[RAD:RAD + height, RAD + offset:RAD + offset + breadth]
            col_flag = col_inside[RAD + offset:RAD + offset + breadth][None, :]
            for neighbour, inside in ((row_near, row_flag), (col_near, col_flag)):
                contrast = neighbour - center
                kernel = jnp.exp(-spatial - contrast * contrast * (0.5 / (SIGMA_RANGE * SIGMA_RANGE))) * inside
                numerator = numerator + kernel * neighbour
                weight = weight + kernel
    return numerator / weight

def reference(pulses, owner, centres):
    blocks = [lax.dynamic_index_in_dim(pulses[block_id], owner[block_id], 0, keepdims=False) for block_id in range(NBLK)]
    tile_cols = N_SUB * TC

    def one_tile(tile_index):
        tile_row = tile_index // N_COL
        tile_col = tile_index % N_COL
        shift_rows = centres[tile_row, tile_col, 0]
        shift_cols = centres[tile_row, tile_col, 1]
        global_rows = tile_row * TR + jnp.arange(TR, dtype=jnp.int32)
        global_cols = tile_col * tile_cols + jnp.arange(tile_cols, dtype=jnp.int32)
        freq_table = range_table(global_cols)
        accumulated = jnp.zeros((TR, 2 * tile_cols), jnp.float32)
        for block_id in range(NBLK):
            global_pulses = block_id * PB + jnp.arange(PB, dtype=jnp.int32)
            accumulated = accumulated + form_block(blocks[block_id], global_pulses, global_rows, freq_table, shift_rows, shift_cols, NR)
        return accumulated
    tile_images = lax.map(one_tile, jnp.arange(N_ROW * N_COL, dtype=jnp.int32))
    tile_images = tile_images.reshape(N_ROW, N_COL, TR, 2, tile_cols)
    formed_image = tile_images.transpose(0, 2, 3, 1, 4).reshape(NR, 2, NC)
    intensity = formed_image[:, 0] * formed_image[:, 0] + formed_image[:, 1] * formed_image[:, 1]
    row_inside = jnp.pad(jnp.ones((NR,), jnp.float32), RAD)
    col_inside = jnp.pad(jnp.ones((NC,), jnp.float32), RAD)
    first_pass = bilateral(jnp.pad(intensity, RAD), row_inside, col_inside)
    despeckled = bilateral(jnp.pad(first_pass, RAD), row_inside, col_inside)
    return (formed_image, despeckled)
```

```python
import math

import jax
import jax.numpy as jnp
import numpy as np
from jax import lax
from jax.experimental import pallas as pl
from jax.experimental.pallas import tpu as pltpu
from jax.sharding import PartitionSpec as P

F = 1024
PB = 256
NBLK = 2
TR = 32
TC = 128
RAD = 16
LANES = 128
CHUNK = 4

SIGMA_RANGE = 1.0
LOG2E = math.log2(math.e)
OUTSIDE = 1.0e18
MESH = pl.DeviceIdType.MESH


def range_table(chip_cols):
    index = np.arange(F)[:, None] * np.arange(chip_cols)[None, :] % F
    angle = 2.0 * np.pi * index / F
    table = np.concatenate([np.cos(angle), -np.sin(angle)], axis=1) / math.sqrt(F)
    return jnp.asarray(table.astype(np.float32), jnp.bfloat16)


def wrap(index, count):
    if count & (count - 1) == 0:
        return index & (count - 1)
    return lax.rem(lax.rem(index, count) + count, count)


def cos_sin(index, count):
    quarters = index.astype(jnp.float32) * (4.0 / count)
    nearest = jnp.floor(quarters + 0.5)
    x = (quarters - nearest) * (0.5 * math.pi)
    x2 = x * x
    sine = x * (1.0 + x2 * (-1.0 / 6 + x2 * (1.0 / 120 + x2 * (-1.0 / 5040))))
    cosine = 1.0 + x2 * (-0.5 + x2 * (1.0 / 24 + x2 * (-1.0 / 720 + x2 * (1.0 / 40320))))
    turn = nearest.astype(jnp.int32)
    odd = (turn & 1) == 1
    base_c = jnp.where(odd, sine, cosine)
    base_s = jnp.where(odd, cosine, sine)
    c = jnp.where(((turn + 1) & 2) == 2, -base_c, base_c)
    s = jnp.where((turn & 2) == 2, -base_s, base_s)
    return c, s


def smooth(field, left, right):
    center = field[RAD : RAD + TR, :]
    lane = lax.broadcasted_iota(jnp.int32, (TR, TC), 1)
    beside = jnp.where(lane < RAD, right[...], left[...])
    numerator = center
    weight = jnp.ones_like(center)
    for distance in range(1, RAD + 1):
        spatial = 2.0 * distance * distance / (RAD * RAD) * LOG2E
        above = field[RAD - distance : RAD - distance + TR, :]
        below = field[RAD + distance : RAD + distance + TR, :]
        after = pltpu.roll(jnp.where(lane < distance, beside, center), TC - distance, 1)
        before = pltpu.roll(jnp.where(lane >= TC - distance, beside, center), distance, 1)
        for near in (above, below, after, before):
            contrast = near - center
            kernel = jnp.exp2(
                -spatial - contrast * contrast * (0.5 * LOG2E / (SIGMA_RANGE * SIGMA_RANGE))
            )
            numerator = numerator + kernel * near
            weight = weight + kernel
    return numerator / weight


def make_kernel(n_rows, n_cols, n_subs):
    all_rows = TR * n_rows
    chip_cols = n_subs * TC
    n_tiles = n_cols * n_subs
    half = PB // n_subs
    chunk = min(CHUNK, n_rows)
    lines = chunk * TR

    def kernel(
        owner_ref, centres_ref, pulses_hbm, table_hbm, image_ref, despeckled_ref,
        pulses, table, shifts, part, part_in, wire, wire_in, fields, lefts, rights,
        load_sem, shift_send, shift_recv, sub_send, sub_recv, row_send, row_recv,
        halo_send, halo_recv,
    ):
        row = lax.axis_index("row")
        col = lax.axis_index("col")
        sub = lax.axis_index("sub")
        place = col * n_subs + sub
        other = 1 - sub

        load_pulses = pltpu.make_async_copy(pulses_hbm, pulses, load_sem.at[0])
        load_table = pltpu.make_async_copy(table_hbm, table, load_sem.at[1])
        load_pulses.start()
        load_table.start()

        for step in range(2):
            fields[step, 0:RAD, :] = jnp.full((RAD, TC), OUTSIDE, jnp.float32)
            fields[step, RAD + TR :, :] = jnp.full((RAD, TC), OUTSIDE, jnp.float32)
            lefts[step] = jnp.full((TR, TC), OUTSIDE, jnp.float32)
            rights[step] = jnp.full((TR, TC), OUTSIDE, jnp.float32)
        packed = centres_ref[0, 0, 0] * 65536 + centres_ref[0, 0, 1]
        shifts[row] = jnp.full((8, LANES), packed, jnp.int32)

        def beside(step):
            where = place + step
            return {"col": where // n_subs, "sub": where % n_subs}

        has_left = place > 0
        has_right = place < n_tiles - 1
        has_above = row > 0
        has_below = row < n_rows - 1

        barrier = pltpu.get_barrier_semaphore()
        for step in range(1, n_rows):
            pl.semaphore_signal(
                barrier, inc=1, device_id={"row": lax.rem(row + step, n_rows)}, device_id_type=MESH
            )

        @pl.when(has_left)
        def _():
            pl.semaphore_signal(barrier, inc=1, device_id=beside(-1), device_id_type=MESH)

        @pl.when(has_right)
        def _():
            pl.semaphore_signal(barrier, inc=1, device_id=beside(1), device_id_type=MESH)

        pl.semaphore_wait(
            barrier, n_rows - 1 + has_left.astype(jnp.int32) + has_right.astype(jnp.int32)
        )

        shift_copies = []
        for step in range(1, n_rows):
            copy = pltpu.make_async_remote_copy(
                src_ref=shifts.at[row],
                dst_ref=shifts.at[row],
                send_sem=shift_send.at[step],
                recv_sem=shift_recv.at[step],
                device_id={"row": lax.rem(row + step, n_rows)},
                device_id_type=MESH,
            )
            copy.start()
            shift_copies.append(copy)
        for copy in shift_copies:
            copy.wait()

        load_pulses.wait()
        load_table.wait()

        mine = [
            jnp.where(owner_ref[block] == row, 1.0 / math.sqrt(NBLK * PB), 0.0)
            for block in range(NBLK)
        ]

        def form(first):
            real_lines, imag_lines = [], []
            lane = lax.broadcasted_iota(jnp.int32, (TR, half), 1)
            line = lax.broadcasted_iota(jnp.int32, (TR, half), 0)
            packs = [shifts[first + tile] for tile in range(chunk)]
            for tile in range(chunk):
                down = jnp.concatenate([packs[tile][:, :1] >> 16] * (TR // 8), axis=0)
                lines_at = (first + tile) * TR + line - down
                real_line, imag_line = [], []
                for block in range(NBLK):
                    pulse = block * PB + sub * half + lane
                    c, s = cos_sin(wrap(pulse * lines_at, all_rows), all_rows)
                    c = (c * mine[block]).astype(jnp.bfloat16)
                    s = (s * mine[block]).astype(jnp.bfloat16)
                    real_line += [c, s]
                    imag_line += [-s, c]
                real_lines.append(jnp.concatenate(real_line, axis=1))
                imag_lines.append(jnp.concatenate(imag_line, axis=1))
            azimuth = jnp.concatenate(real_lines + imag_lines, axis=0)
            focused = jnp.dot(azimuth, pulses[...], preferred_element_type=jnp.float32)
            turned_real, turned_imag = [], []
            for tile in range(chunk):
                across = packs[tile][:, :1] & 65535
                frequency = lax.broadcasted_iota(jnp.int32, (8, F), 1)
                c, s = cos_sin(wrap(frequency * (across - col * chip_cols), F), F)
                c = jnp.concatenate([c] * (TR // 8), axis=0)
                s = jnp.concatenate([s] * (TR // 8), axis=0)
                real = focused[tile * TR : (tile + 1) * TR]
                imag = focused[lines + tile * TR : lines + (tile + 1) * TR]
                turned_real.append((real * c - imag * s).astype(jnp.bfloat16))
                turned_imag.append((real * s + imag * c).astype(jnp.bfloat16))
            turned = jnp.concatenate(turned_real + turned_imag, axis=0)
            product = jnp.dot(turned, table[...], preferred_element_type=jnp.float32)
            real = product[:lines, :chip_cols] - product[lines:, chip_cols:]
            imag = product[:lines, chip_cols:] + product[lines:, :chip_cols]
            for which in range(n_subs):
                for tile in range(chunk):
                    at = slice(tile * TR, (tile + 1) * TR)
                    cut = slice(which * TC, (which + 1) * TC)
                    part[which, first + tile, 0] = real[at, cut]
                    part[which, first + tile, 1] = imag[at, cut]

        if chunk == n_rows:
            form(0)
        else:

            def body(index, carry):
                form(index * chunk)
                return carry

            lax.fori_loop(0, n_rows // chunk, body, 0)

        to_other = pltpu.make_async_remote_copy(
            src_ref=part.at[other],
            dst_ref=part_in,
            send_sem=sub_send,
            recv_sem=sub_recv,
            device_id={"sub": other},
            device_id_type=MESH,
        )
        to_other.start()
        to_other.wait()

        row_copies = []
        for step in range(1, n_rows):
            target = lax.rem(row + step, n_rows)
            wire[step] = (part[sub, target] + part_in[target]).astype(jnp.bfloat16)
            copy = pltpu.make_async_remote_copy(
                src_ref=wire.at[step],
                dst_ref=wire_in.at[step],
                send_sem=row_send.at[step],
                recv_sem=row_recv.at[step],
                device_id={"row": target},
                device_id_type=MESH,
            )
            copy.start()
            row_copies.append(copy)
        image = part[sub, row] + part_in[row]
        for copy in row_copies:
            copy.wait()
        for step in range(1, n_rows):
            image = image + wire_in[step].astype(jnp.float32)
        image_ref[:, 0, :] = image[0]
        image_ref[:, 1, :] = image[1]
        field = image[0] * image[0] + image[1] * image[1]

        for step in range(2):
            fields[step, RAD : RAD + TR, :] = field
            low = fields.at[step, RAD : 2 * RAD]
            high = fields.at[step, TR : RAD + TR]
            whole = fields.at[step, RAD : RAD + TR]
            plans = (
                (has_above, has_below, low, fields.at[step, RAD + TR :], {"row": row - 1}),
                (has_below, has_above, high, fields.at[step, 0:RAD], {"row": row + 1}),
                (has_left, has_right, whole, rights.at[step], beside(-1)),
                (has_right, has_left, whole, lefts.at[step], beside(1)),
            )
            copies = []
            for number, (sends, receives, source, target, device) in enumerate(plans):
                copy = pltpu.make_async_remote_copy(
                    src_ref=source,
                    dst_ref=target,
                    send_sem=halo_send.at[step, number],
                    recv_sem=halo_recv.at[step, number],
                    device_id=device,
                    device_id_type=MESH,
                )
                copies.append((sends, receives, copy))

                @pl.when(sends)
                def _():
                    copy.start()

            for sends, receives, copy in copies:

                @pl.when(receives)
                def _():
                    copy.wait_recv()

            field = smooth(fields.at[step], lefts.at[step], rights.at[step])
            for sends, receives, copy in copies:

                @pl.when(sends)
                def _():
                    copy.wait_send()

        despeckled_ref[...] = field

    dma = pltpu.SemaphoreType.DMA
    vmem = pl.BlockSpec(memory_space=pltpu.VMEM)
    smem = pl.BlockSpec(memory_space=pltpu.SMEM)
    hbm = pl.BlockSpec(memory_space=pl.ANY)
    depth = NBLK * 2 * half
    return pl.pallas_call(
        kernel,
        out_shape=(
            jax.ShapeDtypeStruct((TR, 2, TC), jnp.float32),
            jax.ShapeDtypeStruct((TR, TC), jnp.float32),
        ),
        in_specs=[smem, smem, hbm, hbm],
        out_specs=(vmem, vmem),
        scratch_shapes=[
            pltpu.VMEM((depth, F), jnp.bfloat16),
            pltpu.VMEM((F, 2 * chip_cols), jnp.bfloat16),
            pltpu.VMEM((n_rows, 8, LANES), jnp.int32),
            pltpu.VMEM((n_subs, n_rows, 2, TR, TC), jnp.float32),
            pltpu.VMEM((n_rows, 2, TR, TC), jnp.float32),
            pltpu.VMEM((n_rows, 2, TR, TC), jnp.bfloat16),
            pltpu.VMEM((n_rows, 2, TR, TC), jnp.bfloat16),
            pltpu.VMEM((2, TR + 2 * RAD, TC), jnp.float32),
            pltpu.VMEM((2, TR, TC), jnp.float32),
            pltpu.VMEM((2, TR, TC), jnp.float32),
            dma((2,)),
            dma((n_rows,)),
            dma((n_rows,)),
            dma,
            dma,
            dma((n_rows,)),
            dma((n_rows,)),
            dma((2, 4)),
            dma((2, 4)),
        ],
        compiler_params=pltpu.CompilerParams(
            collective_id=0, has_side_effects=True, vmem_limit_bytes=40 * 2**20
        ),
        cost_estimate=pl.CostEstimate(
            flops=4 * lines * depth * F * 2, bytes_accessed=3 * 2**20, transcendentals=2**20
        ),
    )


def solution(mesh):
    n_rows, n_cols, n_subs = (mesh.shape[name] for name in ("row", "col", "sub"))
    call = make_kernel(n_rows, n_cols, n_subs)
    table = range_table(n_subs * TC)

    def per_device(pulses, owner, centres):
        return call(owner, centres, pulses.reshape(-1, F), table)

    return jax.shard_map(
        per_device,
        mesh=mesh,
        in_specs=(
            P(None, ("groups", "row"), None, "sub", None),
            P("groups"),
            P(("groups", "row"), "col", None),
        ),
        out_specs=(
            P(("groups", "row"), None, ("col", "sub")),
            P(("groups", "row"), ("col", "sub")),
        ),
        check_vma=False,
    )
```

```python
import math

import jax
import jax.numpy as jnp
import numpy as np
from jax import lax
from jax.experimental import pallas as pl
from jax.experimental.pallas import tpu as pltpu
from jax.sharding import PartitionSpec as P

F = 1024
PB = 256
NBLK = 2
TR = 32
TC = 128
RAD = 16
LANES = 128
CHUNK = 4

SIGMA_RANGE = 1.0
LOG2E = math.log2(math.e)
OUTSIDE = 1.0e18
UNIT = math.sqrt(0.5 * LOG2E) / SIGMA_RANGE
MESH = pl.DeviceIdType.MESH


def constant(table):
    return jnp.asarray(table.astype(np.float32), jnp.bfloat16)


def range_table(n_subs):
    index = np.arange(F)[:, None] * np.arange(n_subs * TC)[None, :] % F
    angle = (2.0 * np.pi / F * index).reshape(F, n_subs, TC).transpose(1, 0, 2)
    return constant(np.concatenate([np.cos(angle), -np.sin(angle)], axis=2) / math.sqrt(F))


def azimuth_table(all_rows, n_subs):
    index = np.arange(all_rows)[:, None] * np.arange(NBLK * PB)[None, :] % all_rows
    angle = (2.0 * np.pi / all_rows * index).reshape(all_rows, NBLK, n_subs, PB // n_subs)
    c = np.cos(angle).transpose(2, 0, 1, 3)
    s = np.sin(angle).transpose(2, 0, 1, 3)
    parts = [np.stack([c, s], axis=3), np.stack([-s, c], axis=3)]
    table = np.concatenate([part.reshape(n_subs, all_rows, -1) for part in parts], axis=1)
    return constant(table / math.sqrt(NBLK * PB))


def cos_sin(index, count):
    quarters = index.astype(jnp.float32) * (4.0 / count)
    nearest = jnp.floor(quarters + 0.5)
    x = (quarters - nearest) * (0.5 * math.pi)
    x2 = x * x
    sine = x * (1.0 + x2 * (-1.0 / 6 + x2 * (1.0 / 120 + x2 * (-1.0 / 5040))))
    cosine = 1.0 + x2 * (-0.5 + x2 * (1.0 / 24 + x2 * (-1.0 / 720 + x2 * (1.0 / 40320))))
    turn = nearest.astype(jnp.int32)
    odd = (turn & 1) == 1
    base_c = jnp.where(odd, sine, cosine)
    base_s = jnp.where(odd, cosine, sine)
    c = jnp.where(((turn + 1) & 2) == 2, -base_c, base_c)
    s = jnp.where((turn & 2) == 2, -base_s, base_s)
    return c, s


def smooth(field, left, right):
    center = field[RAD : RAD + TR, :]
    lane = lax.broadcasted_iota(jnp.int32, (TR, TC), 1)
    beside = jnp.where(lane < RAD, right[...], left[...])
    numerator = center
    weight = jnp.ones_like(center)
    for distance in range(1, RAD + 1):
        spatial = 2.0 * distance * distance / (RAD * RAD) * LOG2E
        above = field[RAD - distance : RAD - distance + TR, :]
        below = field[RAD + distance : RAD + distance + TR, :]
        after = pltpu.roll(jnp.where(lane < distance, beside, center), TC - distance, 1)
        before = pltpu.roll(jnp.where(lane >= TC - distance, beside, center), distance, 1)
        for near in (above, below, after, before):
            contrast = near - center
            kernel = jnp.exp2(-spatial - contrast * contrast)
            numerator = numerator + kernel * near
            weight = weight + kernel
    return numerator / weight


def make_kernel(n_rows, n_cols, n_subs):
    all_rows = TR * n_rows
    chip_cols = n_subs * TC
    n_tiles = n_cols * n_subs
    half = PB // n_subs
    depth = NBLK * 2 * half
    chunk = min(CHUNK, n_rows)
    lines = chunk * TR

    def kernel(
        owner_hbm, centres_hbm, pulses_hbm, azimuth_hbm, table_hbm, image_ref, despeckled_ref,
        owner, centres, pulses, azimuth, table, focused_real, focused_imag, shifts, part, part_in, wire, wire_in, fields, lefts, rights,
        load_sem, shift_send, shift_recv, sub_send, sub_recv, row_send, row_recv,
        halo_send, halo_recv,
    ):
        row = lax.axis_index("row")
        col = lax.axis_index("col")
        sub = lax.axis_index("sub")
        place = col * n_subs + sub
        other = 1 - sub

        loads = [
            pltpu.make_async_copy(source, target, load_sem.at[number])
            for number, (source, target) in enumerate(
                (
                    (centres_hbm, centres),
                    (owner_hbm, owner),
                    (azimuth_hbm.at[sub], azimuth),
                    (pulses_hbm, pulses),
                    (table_hbm, table),
                )
            )
        ]
        load_centres, load_owner, load_azimuth, load_pulses, load_table = loads
        for load in loads:
            load.start()

        for step in range(2):
            fields[step, 0:RAD, :] = jnp.full((RAD, TC), OUTSIDE, jnp.float32)
            fields[step, RAD + TR :, :] = jnp.full((RAD, TC), OUTSIDE, jnp.float32)
            lefts[step] = jnp.full((TR, TC), OUTSIDE, jnp.float32)
            rights[step] = jnp.full((TR, TC), OUTSIDE, jnp.float32)
        def beside(step):
            where = place + step
            return {"col": where // n_subs, "sub": where % n_subs}

        has_left = place > 0
        has_right = place < n_tiles - 1
        has_above = row > 0
        has_below = row < n_rows - 1

        barrier = pltpu.get_barrier_semaphore()
        for step in range(1, n_rows):
            pl.semaphore_signal(
                barrier, inc=1, device_id={"row": lax.rem(row + step, n_rows)}, device_id_type=MESH
            )

        @pl.when(has_left)
        def _():
            pl.semaphore_signal(barrier, inc=1, device_id=beside(-1), device_id_type=MESH)

        @pl.when(has_right)
        def _():
            pl.semaphore_signal(barrier, inc=1, device_id=beside(1), device_id_type=MESH)

        load_centres.wait()
        packed = centres[0, 0, 0] * 65536 + centres[0, 0, 1]
        shifts[row] = jnp.full((8, LANES), packed, jnp.int32)

        pl.semaphore_wait(
            barrier, n_rows - 1 + has_left.astype(jnp.int32) + has_right.astype(jnp.int32)
        )

        shift_copies = []
        for step in range(1, n_rows):
            copy = pltpu.make_async_remote_copy(
                src_ref=shifts.at[row],
                dst_ref=shifts.at[row],
                send_sem=shift_send.at[step],
                recv_sem=shift_recv.at[step],
                device_id={"row": lax.rem(row + step, n_rows)},
                device_id_type=MESH,
            )
            copy.start()
            shift_copies.append(copy)

        load_owner.wait()
        load_azimuth.wait()
        which_block = lax.broadcasted_iota(jnp.int32, (1, depth), 1) // (2 * half)
        mine = jnp.zeros((1, depth), jnp.float32)
        for block in range(NBLK):
            held = jnp.where(owner[block] == row, 1.0, 0.0)
            mine = jnp.where(which_block == block, held, mine)
        masked = azimuth[...] * mine.astype(jnp.bfloat16)
        load_pulses.wait()
        focused = jnp.dot(masked, pulses[...], preferred_element_type=jnp.float32)
        for target, values in (
            (focused_real, focused[:all_rows]), (focused_imag, focused[all_rows:])
        ):
            for group in range(F // LANES):
                cut = values[:, group * LANES : (group + 1) * LANES]
                target[group, TR:, :] = cut
                target[group, 0:TR, :] = cut[all_rows - TR :]

        for copy in shift_copies:
            copy.wait()
        load_table.wait()

        def turn(first):
            turned_real, turned_imag = [], []
            for tile in range(chunk):
                pack = shifts[first + tile]
                down = pack[0, 0] >> 16
                across = (pack[:, :1] & 65535) - col * chip_cols
                frequency = lax.broadcasted_iota(jnp.int32, (8, F), 1)
                c, s = cos_sin((frequency * across) & (F - 1), F)
                c = jnp.concatenate([c] * (TR // 8), axis=0)
                s = jnp.concatenate([s] * (TR // 8), axis=0)
                at = pl.ds((first + tile + 1) * TR - down, TR)
                groups = range(F // LANES)
                real = jnp.concatenate([focused_real[group, at, :] for group in groups], axis=1)
                imag = jnp.concatenate([focused_imag[group, at, :] for group in groups], axis=1)
                turned_real.append((real * c - imag * s).astype(jnp.bfloat16))
                turned_imag.append((real * s + imag * c).astype(jnp.bfloat16))
            return jnp.concatenate(turned_real + turned_imag, axis=0)

        def form(turned, first, which):
            product = jnp.dot(turned, table[which], preferred_element_type=jnp.float32)
            real = product[:lines, :TC] - product[lines:, TC:]
            imag = product[:lines, TC:] + product[lines:, :TC]
            for tile in range(chunk):
                at = slice(tile * TR, (tile + 1) * TR)
                part[which, first + tile, 0] = real[at]
                part[which, first + tile, 1] = imag[at]

        to_other = pltpu.make_async_remote_copy(
            src_ref=part.at[other],
            dst_ref=part_in,
            send_sem=sub_send,
            recv_sem=sub_recv,
            device_id={"sub": other},
            device_id_type=MESH,
        )
        if chunk == n_rows:
            turned = turn(0)
            form(turned, 0, other)
            to_other.start()
            form(turned, 0, sub)
        else:

            def body(index, carry):
                turned = turn(index * chunk)
                form(turned, index * chunk, other)
                form(turned, index * chunk, sub)
                return carry

            lax.fori_loop(0, n_rows // chunk, body, 0)
            to_other.start()
        to_other.wait()

        row_copies = []
        for step in range(1, n_rows):
            target = lax.rem(row + step, n_rows)
            wire[step] = (part[sub, target] + part_in[target]).astype(jnp.bfloat16)
            copy = pltpu.make_async_remote_copy(
                src_ref=wire.at[step],
                dst_ref=wire_in.at[step],
                send_sem=row_send.at[step],
                recv_sem=row_recv.at[step],
                device_id={"row": target},
                device_id_type=MESH,
            )
            copy.start()
            row_copies.append(copy)
        image = part[sub, row] + part_in[row]
        for copy in row_copies:
            copy.wait()
        for step in range(1, n_rows):
            image = image + wire_in[step].astype(jnp.float32)
        image_ref[:, 0, :] = image[0]
        image_ref[:, 1, :] = image[1]
        field = (image[0] * image[0] + image[1] * image[1]) * UNIT

        for step in range(2):
            fields[step, RAD : RAD + TR, :] = field
            low = fields.at[step, RAD : 2 * RAD]
            high = fields.at[step, TR : RAD + TR]
            whole = fields.at[step, RAD : RAD + TR]
            plans = (
                (has_above, has_below, low, fields.at[step, RAD + TR :], {"row": row - 1}),
                (has_below, has_above, high, fields.at[step, 0:RAD], {"row": row + 1}),
                (has_left, has_right, whole, rights.at[step], beside(-1)),
                (has_right, has_left, whole, lefts.at[step], beside(1)),
            )
            copies = []
            for number, (sends, receives, source, target, device) in enumerate(plans):
                copy = pltpu.make_async_remote_copy(
                    src_ref=source,
                    dst_ref=target,
                    send_sem=halo_send.at[step, number],
                    recv_sem=halo_recv.at[step, number],
                    device_id=device,
                    device_id_type=MESH,
                )
                copies.append((sends, receives, copy))

                @pl.when(sends)
                def _():
                    copy.start()

            for sends, receives, copy in copies:

                @pl.when(receives)
                def _():
                    copy.wait_recv()

            field = smooth(fields.at[step], lefts.at[step], rights.at[step])
            for sends, receives, copy in copies:

                @pl.when(sends)
                def _():
                    copy.wait_send()

        despeckled_ref[...] = field * (1.0 / UNIT)

    dma = pltpu.SemaphoreType.DMA
    vmem = pl.BlockSpec(memory_space=pltpu.VMEM)
    hbm = pl.BlockSpec(memory_space=pltpu.HBM)
    return pl.pallas_call(
        kernel,
        out_shape=(
            jax.ShapeDtypeStruct((TR, 2, TC), jnp.float32),
            jax.ShapeDtypeStruct((TR, TC), jnp.float32),
        ),
        in_specs=[hbm] * 5,
        out_specs=(vmem, vmem),
        scratch_shapes=[
            pltpu.SMEM((NBLK,), jnp.int32),
            pltpu.SMEM((1, 1, 2), jnp.int32),
            pltpu.VMEM((depth, F), jnp.bfloat16),
            pltpu.VMEM((2 * all_rows, depth), jnp.bfloat16),
            pltpu.VMEM((n_subs, F, 2 * TC), jnp.bfloat16),
            pltpu.VMEM((F // LANES, TR + all_rows, LANES), jnp.float32),
            pltpu.VMEM((F // LANES, TR + all_rows, LANES), jnp.float32),
            pltpu.VMEM((n_rows, 8, LANES), jnp.int32),
            pltpu.VMEM((n_subs, n_rows, 2, TR, TC), jnp.float32),
            pltpu.VMEM((n_rows, 2, TR, TC), jnp.float32),
            pltpu.VMEM((n_rows, 2, TR, TC), jnp.bfloat16),
            pltpu.VMEM((n_rows, 2, TR, TC), jnp.bfloat16),
            pltpu.VMEM((2, TR + 2 * RAD, TC), jnp.float32),
            pltpu.VMEM((2, TR, TC), jnp.float32),
            pltpu.VMEM((2, TR, TC), jnp.float32),
            dma((5,)),
            dma((n_rows,)),
            dma((n_rows,)),
            dma,
            dma,
            dma((n_rows,)),
            dma((n_rows,)),
            dma((2, 4)),
            dma((2, 4)),
        ],
        compiler_params=pltpu.CompilerParams(
            collective_id=0, has_side_effects=True, vmem_limit_bytes=60 * 2**20
        ),
        cost_estimate=pl.CostEstimate(
            flops=4 * lines * depth * F * 2, bytes_accessed=3 * 2**20, transcendentals=2**20
        ),
    )


def solution(mesh):
    n_rows, n_cols, n_subs = (mesh.shape[name] for name in ("row", "col", "sub"))
    call = make_kernel(n_rows, n_cols, n_subs)
    azimuth = azimuth_table(TR * n_rows, n_subs)
    table = range_table(n_subs)

    def per_device(pulses, owner, centres):
        return call(owner, centres, pulses.reshape(-1, F), azimuth, table)

    return jax.shard_map(
        per_device,
        mesh=mesh,
        in_specs=(
            P(None, ("groups", "row"), None, "sub", None),
            P("groups"),
            P(("groups", "row"), "col", None),
        ),
        out_specs=(
            P(("groups", "row"), None, ("col", "sub")),
            P(("groups", "row"), ("col", "sub")),
        ),
        check_vma=False,
    )
```

```python
import math

import jax
import jax.numpy as jnp
import numpy as np
from jax import lax
from jax.experimental import pallas as pl
from jax.experimental.pallas import tpu as pltpu
from jax.sharding import PartitionSpec as P

F = 1024
PB = 256
NBLK = 2
TR = 32
TC = 128
RAD = 16
LANES = 128
CHUNK = 4

SIGMA_RANGE = 1.0
LOG2E = math.log2(math.e)
OUTSIDE = 1.0e18
UNIT = math.sqrt(0.5 * LOG2E) / SIGMA_RANGE
MESH = pl.DeviceIdType.MESH


def constant(table):
    return jnp.asarray(table.astype(np.float32), jnp.bfloat16)


def range_table(n_subs):
    index = np.arange(F)[:, None] * np.arange(n_subs * TC)[None, :] % F
    angle = (2.0 * np.pi / F * index).reshape(F, n_subs, TC).transpose(1, 0, 2)
    return constant(np.concatenate([np.cos(angle), -np.sin(angle)], axis=2) / math.sqrt(F))


def azimuth_table(all_rows, n_subs):
    index = np.arange(all_rows)[:, None] * np.arange(NBLK * PB)[None, :] % all_rows
    angle = (2.0 * np.pi / all_rows * index).reshape(all_rows, NBLK, n_subs, PB // n_subs)
    c = np.cos(angle).transpose(2, 0, 1, 3)
    s = np.sin(angle).transpose(2, 0, 1, 3)
    parts = [np.stack([c, s], axis=3), np.stack([-s, c], axis=3)]
    table = np.concatenate([part.reshape(n_subs, all_rows, -1) for part in parts], axis=1)
    return constant(table / math.sqrt(NBLK * PB))


def cos_sin(index, count):
    quarters = index.astype(jnp.float32) * (4.0 / count)
    nearest = jnp.floor(quarters + 0.5)
    x = (quarters - nearest) * (0.5 * math.pi)
    x2 = x * x
    sine = x * (1.0 + x2 * (-1.0 / 6 + x2 * (1.0 / 120 + x2 * (-1.0 / 5040))))
    cosine = 1.0 + x2 * (-0.5 + x2 * (1.0 / 24 + x2 * (-1.0 / 720 + x2 * (1.0 / 40320))))
    turn = nearest.astype(jnp.int32)
    odd = (turn & 1) == 1
    base_c = jnp.where(odd, sine, cosine)
    base_s = jnp.where(odd, cosine, sine)
    c = jnp.where(((turn + 1) & 2) == 2, -base_c, base_c)
    s = jnp.where((turn & 2) == 2, -base_s, base_s)
    return c, s


def add(sums, near, center, spatial):
    contrast = near - center
    kernel = jnp.exp2(-spatial - contrast * contrast)
    return sums[0] + kernel * near, sums[1] + kernel


SPATIAL = [2.0 * d * d / (RAD * RAD) * LOG2E for d in range(RAD + 1)]


def begin(field):
    centers = [field[RAD + first : RAD + first + 8, :] for first in range(0, TR, 8)]
    return [(center, jnp.ones_like(center)) for center in centers]


def along_rows(field, sums, inner):
    result = []
    for number, first in enumerate(range(0, TR, 8)):
        center = field[RAD + first : RAD + first + 8, :]
        total = sums[number]
        for distance in range(1, RAD + 1):
            for low in (first - distance, first + distance):
                if (0 <= low <= TR - 8) == inner:
                    near = field[RAD + low : RAD + low + 8, :]
                    total = add(total, near, center, SPATIAL[distance])
        result.append(total)
    return result


def along_cols(field, outer, sums):
    result = []
    lane = lax.broadcasted_iota(jnp.int32, (8, TC), 1)
    for number, first in enumerate(range(0, TR, 8)):
        center = field[RAD + first : RAD + first + 8, :]
        outside = outer[first : first + 8, :]
        total = sums[number]
        for distance in range(1, RAD + 1):
            after = pltpu.roll(jnp.where(lane < distance, outside, center), TC - distance, 1)
            before = pltpu.roll(jnp.where(lane >= TC - distance, outside, center), distance, 1)
            for near in (after, before):
                total = add(total, near, center, SPATIAL[distance])
        result.append(total)
    return result


def ratio(sums):
    return jnp.concatenate([numerator / weight for numerator, weight in sums], axis=0)


def last_pass(packed, image_hbm, despeckled_ref, image, image_sem):
    image[:, 0, :] = packed[0:TR, :]
    image[:, 1, :] = packed[TR : 2 * TR, :]
    copy = pltpu.make_async_copy(image, image_hbm, image_sem)
    copy.start()
    field = packed.at[2 * TR : 4 * TR]
    outer = packed[4 * TR : 5 * TR, :]
    sums = along_rows(field, begin(field), True)
    sums = along_rows(field, sums, False)
    sums = along_cols(field, outer, sums)
    despeckled_ref[...] = ratio(sums) * (1.0 / UNIT)
    copy.wait()


def make_kernel(n_rows, n_cols, n_subs):
    all_rows = TR * n_rows
    chip_cols = n_subs * TC
    n_tiles = n_cols * n_subs
    half = PB // n_subs
    depth = NBLK * 2 * half
    chunk = min(CHUNK, n_rows)
    lines = chunk * TR

    def kernel(
        owner_hbm, centres_hbm, pulses_hbm, azimuth_hbm, table_hbm, packed_ref,
        owner, centres, pulses, pulses_in, azimuth, table, focused_real, focused_imag, shifts, part, wire, wire_in, fields, lefts, rights,
        load_sem, shift_send, shift_recv, sub_send, sub_recv, row_send, row_recv,
        halo_send, halo_recv,
    ):
        row = lax.axis_index("row")
        col = lax.axis_index("col")
        sub = lax.axis_index("sub")
        place = col * n_subs + sub
        other = 1 - sub

        loads = [
            pltpu.make_async_copy(source, target, load_sem.at[number])
            for number, (source, target) in enumerate(
                (
                    (centres_hbm, centres),
                    (owner_hbm, owner),
                    (azimuth_hbm, azimuth),
                    (pulses_hbm, pulses),
                    (table_hbm.at[sub], table),
                )
            )
        ]
        load_centres, load_owner, load_azimuth, load_pulses, load_table = loads
        for load in loads:
            load.start()

        for step in range(2):
            fields[step, 0:RAD, :] = jnp.full((RAD, TC), OUTSIDE, jnp.float32)
            fields[step, RAD + TR :, :] = jnp.full((RAD, TC), OUTSIDE, jnp.float32)
            lefts[step] = jnp.full((TR, TC), OUTSIDE, jnp.float32)
            rights[step] = jnp.full((TR, TC), OUTSIDE, jnp.float32)
        def beside(step):
            where = place + step
            return {"col": where // n_subs, "sub": where % n_subs}

        has_left = place > 0
        has_right = place < n_tiles - 1
        has_above = row > 0
        has_below = row < n_rows - 1

        barrier = pltpu.get_barrier_semaphore()
        for step in range(1, n_rows):
            pl.semaphore_signal(
                barrier, inc=1, device_id={"row": lax.rem(row + step, n_rows)}, device_id_type=MESH
            )

        @pl.when(has_left)
        def _():
            pl.semaphore_signal(barrier, inc=1, device_id=beside(-1), device_id_type=MESH)

        @pl.when(has_right)
        def _():
            pl.semaphore_signal(barrier, inc=1, device_id=beside(1), device_id_type=MESH)

        load_centres.wait()
        packed = centres[0, 0, 0] * 65536 + centres[0, 0, 1]
        shifts[row] = jnp.full((8, LANES), packed, jnp.int32)

        pl.semaphore_wait(
            barrier, n_rows - 1 + has_left.astype(jnp.int32) + has_right.astype(jnp.int32)
        )

        shift_copies = []
        for step in range(1, n_rows):
            copy = pltpu.make_async_remote_copy(
                src_ref=shifts.at[row],
                dst_ref=shifts.at[row],
                send_sem=shift_send.at[step],
                recv_sem=shift_recv.at[step],
                device_id={"row": lax.rem(row + step, n_rows)},
                device_id_type=MESH,
            )
            copy.start()
            shift_copies.append(copy)

        to_other = pltpu.make_async_remote_copy(
            src_ref=pulses_hbm,
            dst_ref=pulses_in,
            send_sem=sub_send,
            recv_sem=sub_recv,
            device_id={"sub": other},
            device_id_type=MESH,
        )
        to_other.start()

        load_owner.wait()
        load_azimuth.wait()
        which_block = lax.broadcasted_iota(jnp.int32, (1, depth), 1) // (2 * half)
        mine = jnp.zeros((1, depth), jnp.float32)
        for block in range(NBLK):
            held = jnp.where(owner[block] == row, 1.0, 0.0)
            mine = jnp.where(which_block == block, held, mine)
        mine = mine.astype(jnp.bfloat16)
        load_pulses.wait()
        focused = jnp.dot(azimuth[sub] * mine, pulses[...], preferred_element_type=jnp.float32)
        halves = ((focused_real, slice(0, all_rows)), (focused_imag, slice(all_rows, None)))
        for target, at in halves:
            for group in range(F // LANES):
                target[group, TR:, :] = focused[at, group * LANES : (group + 1) * LANES]
        to_other.wait_recv()
        focused = jnp.dot(azimuth[other] * mine, pulses_in[...], preferred_element_type=jnp.float32)
        for target, at in halves:
            for group in range(F // LANES):
                total = target[group, TR:, :] + focused[at, group * LANES : (group + 1) * LANES]
                target[group, TR:, :] = total
                target[group, 0:TR, :] = total[all_rows - TR :]

        load_table.wait()
        for copy in shift_copies:
            copy.wait_recv()

        def turn(first):
            turned_real, turned_imag = [], []
            for tile in range(chunk):
                pack = shifts[first + tile]
                down = pack[0, 0] >> 16
                across = (pack[:, :1] & 65535) - col * chip_cols
                frequency = lax.broadcasted_iota(jnp.int32, (8, F), 1)
                c, s = cos_sin((frequency * across) & (F - 1), F)
                c = jnp.concatenate([c] * (TR // 8), axis=0)
                s = jnp.concatenate([s] * (TR // 8), axis=0)
                at = pl.ds((first + tile + 1) * TR - down, TR)
                groups = range(F // LANES)
                real = jnp.concatenate([focused_real[group, at, :] for group in groups], axis=1)
                imag = jnp.concatenate([focused_imag[group, at, :] for group in groups], axis=1)
                turned_real.append((real * c - imag * s).astype(jnp.bfloat16))
                turned_imag.append((real * s + imag * c).astype(jnp.bfloat16))
            return jnp.concatenate(turned_real + turned_imag, axis=0)

        def form(first):
            product = jnp.dot(turn(first), table[...], preferred_element_type=jnp.float32)
            real = product[:lines, :TC] - product[lines:, TC:]
            imag = product[:lines, TC:] + product[lines:, :TC]
            for tile in range(chunk):
                at = slice(tile * TR, (tile + 1) * TR)
                part[first + tile, 0] = real[at]
                part[first + tile, 1] = imag[at]
                wire[first + tile, 0] = real[at].astype(jnp.bfloat16)
                wire[first + tile, 1] = imag[at].astype(jnp.bfloat16)

        if chunk == n_rows:
            form(0)
        else:

            def body(index, carry):
                form(index * chunk)
                return carry

            lax.fori_loop(0, n_rows // chunk, body, 0)

        row_copies = []
        for step in range(1, n_rows):
            target = lax.rem(row + step, n_rows)
            copy = pltpu.make_async_remote_copy(
                src_ref=wire.at[target],
                dst_ref=wire_in.at[step],
                send_sem=row_send.at[step],
                recv_sem=row_recv.at[step],
                device_id={"row": target},
                device_id_type=MESH,
            )
            copy.start()
            row_copies.append(copy)
        image = part[row]
        for step, copy in enumerate(row_copies, 1):
            copy.wait_recv()
            image = image + wire_in[step].astype(jnp.float32)
        field = (image[0] * image[0] + image[1] * image[1]) * UNIT

        sent = []

        def exchange(step, field):
            fields[step, RAD : RAD + TR, :] = field
            low = fields.at[step, RAD : 2 * RAD]
            high = fields.at[step, TR : RAD + TR]
            whole = fields.at[step, RAD : RAD + TR]
            plans = (
                (has_left, has_right, whole, rights.at[step], beside(-1)),
                (has_right, has_left, whole, lefts.at[step], beside(1)),
                (has_above, has_below, low, fields.at[step, RAD + TR :], {"row": row - 1}),
                (has_below, has_above, high, fields.at[step, 0:RAD], {"row": row + 1}),
            )
            arriving = []
            for number, (sends, receives, source, target, device) in enumerate(plans):
                copy = pltpu.make_async_remote_copy(
                    src_ref=source,
                    dst_ref=target,
                    send_sem=halo_send.at[step, number],
                    recv_sem=halo_recv.at[step, number],
                    device_id=device,
                    device_id_type=MESH,
                )
                sent.append((sends, copy))
                arriving.append((receives, copy))

                @pl.when(sends)
                def _():
                    copy.start()

            return arriving

        def arrive(arriving):
            for receives, copy in arriving:

                @pl.when(receives)
                def _():
                    copy.wait_recv()

        line = lax.broadcasted_iota(jnp.int32, (TR, TC), 1)
        arriving = exchange(0, field)
        packed_ref[0:TR, :] = image[0]
        packed_ref[TR : 2 * TR, :] = image[1]
        first = fields.at[0]
        sums = along_rows(first, begin(first), True)
        arrive(arriving)
        sums = along_rows(first, sums, False)
        outer = jnp.where(line < RAD, rights[0], lefts[0])
        field = ratio(along_cols(first, outer, sums))

        arriving = exchange(1, field)
        to_other.wait_send()
        for copy in shift_copies + row_copies:
            copy.wait_send()
        arrive(arriving)
        packed_ref[2 * TR : 4 * TR, :] = fields[1]
        packed_ref[4 * TR :, :] = jnp.where(line < RAD, rights[1], lefts[1])
        for sends, copy in sent:

            @pl.when(sends)
            def _():
                copy.wait_send()

    dma = pltpu.SemaphoreType.DMA
    vmem = pl.BlockSpec(memory_space=pltpu.VMEM)
    hbm = pl.BlockSpec(memory_space=pltpu.HBM)
    form_call = pl.pallas_call(
        kernel,
        out_shape=jax.ShapeDtypeStruct((5 * TR, TC), jnp.float32),
        in_specs=[hbm] * 5,
        out_specs=vmem,
        scratch_shapes=[
            pltpu.SMEM((NBLK,), jnp.int32),
            pltpu.SMEM((1, 1, 2), jnp.int32),
            pltpu.VMEM((depth, F), jnp.bfloat16),
            pltpu.VMEM((depth, F), jnp.bfloat16),
            pltpu.VMEM((n_subs, 2 * all_rows, depth), jnp.bfloat16),
            pltpu.VMEM((F, 2 * TC), jnp.bfloat16),
            pltpu.VMEM((F // LANES, TR + all_rows, LANES), jnp.float32),
            pltpu.VMEM((F // LANES, TR + all_rows, LANES), jnp.float32),
            pltpu.VMEM((n_rows, 8, LANES), jnp.int32),
            pltpu.VMEM((n_rows, 2, TR, TC), jnp.float32),
            pltpu.VMEM((n_rows, 2, TR, TC), jnp.bfloat16),
            pltpu.VMEM((n_rows, 2, TR, TC), jnp.bfloat16),
            pltpu.VMEM((2, TR + 2 * RAD, TC), jnp.float32),
            pltpu.VMEM((2, TR, TC), jnp.float32),
            pltpu.VMEM((2, TR, TC), jnp.float32),
            dma((5,)),
            dma((n_rows,)),
            dma((n_rows,)),
            dma,
            dma,
            dma((n_rows,)),
            dma((n_rows,)),
            dma((2, 4)),
            dma((2, 4)),
        ],
        compiler_params=pltpu.CompilerParams(
            collective_id=0, has_side_effects=True, vmem_limit_bytes=int(53.5 * 2**20)
        ),
        cost_estimate=pl.CostEstimate(
            flops=4 * lines * depth * F * 2, bytes_accessed=3 * 2**20, transcendentals=2**20
        ),
    )
    last_call = pl.pallas_call(
        last_pass,
        out_shape=(
            jax.ShapeDtypeStruct((TR, 2, TC), jnp.float32),
            jax.ShapeDtypeStruct((TR, TC), jnp.float32),
        ),
        in_specs=[vmem],
        out_specs=(hbm, vmem),
        scratch_shapes=[pltpu.VMEM((TR, 2, TC), jnp.float32), dma],
        cost_estimate=pl.CostEstimate(flops=2**20, bytes_accessed=2**17, transcendentals=2**18),
    )
    return form_call, last_call


def solution(mesh):
    n_rows, n_cols, n_subs = (mesh.shape[name] for name in ("row", "col", "sub"))
    form_call, last_call = make_kernel(n_rows, n_cols, n_subs)
    azimuth = azimuth_table(TR * n_rows, n_subs)
    table = range_table(n_subs)

    def per_device(pulses, owner, centres):
        return last_call(form_call(owner, centres, pulses.reshape(-1, F), azimuth, table))

    return jax.shard_map(
        per_device,
        mesh=mesh,
        in_specs=(
            P(None, ("groups", "row"), None, "sub", None),
            P("groups"),
            P(("groups", "row"), "col", None),
        ),
        out_specs=(
            P(("groups", "row"), None, ("col", "sub")),
            P(("groups", "row"), ("col", "sub")),
        ),
        check_vma=False,
    )
```

```python
import math

import jax
import jax.numpy as jnp
import numpy as np
from jax import lax
from jax.experimental import pallas as pl
from jax.experimental.pallas import tpu as pltpu
from jax.sharding import PartitionSpec as P

F = 1024
PB = 256
NBLK = 2
TR = 32
TC = 128
RAD = 16
LANES = 128

SIGMA_RANGE = 1.0
LOG2E = math.log2(math.e)
OUTSIDE = 1.0e18
UNIT = math.sqrt(0.5 * LOG2E) / SIGMA_RANGE
MESH = pl.DeviceIdType.MESH


def constant(table):
    return jnp.asarray(table.astype(np.float32), jnp.bfloat16)


def range_table():
    index = np.arange(F)[:, None] * np.arange(F)[None, :] % F
    angle = (2.0 * np.pi / F * index).reshape(F, F // TC, TC).transpose(1, 0, 2)
    return constant(np.concatenate([np.cos(angle), -np.sin(angle)], axis=2) / math.sqrt(F))


def azimuth_table(all_rows, n_subs):
    index = np.arange(all_rows)[:, None] * np.arange(NBLK * PB)[None, :] % all_rows
    angle = (2.0 * np.pi / all_rows * index).reshape(all_rows, NBLK, n_subs, PB // n_subs)
    c = np.cos(angle).transpose(2, 0, 1, 3)
    s = np.sin(angle).transpose(2, 0, 1, 3)
    parts = [np.stack([c, s], axis=3), np.stack([-s, c], axis=3)]
    table = np.concatenate([part.reshape(n_subs, all_rows, -1) for part in parts], axis=1)
    return constant(table / math.sqrt(NBLK * PB))


def add(sums, nears, center, distance):
    top = bottom = None
    for near in nears:
        contrast = near - center
        kernel = jnp.exp2(-SPATIAL[distance] - contrast * contrast)
        term = kernel * near
        top = term if top is None else top + term
        bottom = kernel if bottom is None else bottom + kernel
    return (sums[0] + top, sums[1] + bottom) if nears else sums


SPATIAL = [2.0 * d * d / (RAD * RAD) * LOG2E for d in range(RAD + 1)]


def begin(field):
    centers = [field[RAD + first : RAD + first + 8, :] for first in range(0, TR, 8)]
    return [(center, jnp.ones_like(center)) for center in centers]


def along_rows(field, sums, inner):
    sums = list(sums)
    centers = [field[RAD + first : RAD + first + 8, :] for first in range(0, TR, 8)]
    for distance in range(1, RAD + 1):
        for number, first in enumerate(range(0, TR, 8)):
            nears = [
                field[RAD + low : RAD + low + 8, :]
                for low in (first - distance, first + distance)
                if (0 <= low <= TR - 8) == inner
            ]
            sums[number] = add(sums[number], nears, centers[number], distance)
    return sums


def along_cols(field, outer, sums):
    sums = list(sums)
    lane = lax.broadcasted_iota(jnp.int32, (8, TC), 1)
    centers = [field[RAD + first : RAD + first + 8, :] for first in range(0, TR, 8)]
    outers = [outer[first : first + 8, :] for first in range(0, TR, 8)]
    for distance in range(1, RAD + 1):
        for number, (center, outside) in enumerate(zip(centers, outers)):
            after = jnp.where(lane < distance, outside, center)
            before = jnp.where(lane >= TC - distance, outside, center)
            nears = [
                pltpu.roll(after, TC - distance, 1),
                pltpu.roll(before, distance, 1),
            ]
            sums[number] = add(sums[number], nears, center, distance)
    return sums


def ratio(sums):
    return jnp.concatenate([numerator / weight for numerator, weight in sums], axis=0)


def last_pass(packed, image_hbm, despeckled_hbm, image, despeckled, sems):
    image[:, 0, :] = packed[0:TR, :]
    image[:, 1, :] = packed[TR : 2 * TR, :]
    save_image = pltpu.make_async_copy(image, image_hbm, sems.at[0])
    save_image.start()
    field = packed.at[2 * TR : 4 * TR]
    outer = packed[4 * TR : 5 * TR, :]
    sums = along_rows(field, begin(field), True)
    sums = along_rows(field, sums, False)
    sums = along_cols(field, outer, sums)
    despeckled[...] = ratio(sums) * (1.0 / UNIT)
    save = pltpu.make_async_copy(despeckled, despeckled_hbm, sems.at[1])
    save.start()
    save_image.wait()
    save.wait()


def make_kernel(n_rows, n_cols, n_subs):
    all_rows = TR * n_rows
    n_tiles = n_cols * n_subs
    half = PB // n_subs
    depth = NBLK * 2 * half

    def kernel(
        owner_hbm, centres_hbm, pulses_hbm, azimuth_hbm, table_hbm, packed_ref,
        owner, centres, pulses, azimuth, table, focus, focus_out, focus_in, formed, shifts, wire, wire_in, fields, lefts, rights,
        load_sem, shift_send, shift_recv, sub_send, sub_recv, row_send, row_recv,
        halo_send, halo_recv,
    ):
        row = lax.axis_index("row")
        col = lax.axis_index("col")
        sub = lax.axis_index("sub")
        place = col * n_subs + sub
        other = 1 - sub

        loads = [
            pltpu.make_async_copy(source, target, load_sem.at[number])
            for number, (source, target) in enumerate(
                (
                    (centres_hbm, centres),
                    (owner_hbm, owner),
                    (azimuth_hbm.at[sub], azimuth),
                    (pulses_hbm, pulses),
                    (table_hbm.at[lax.rem(place + F // TC - 1, F // TC)], table.at[0]),
                    (table_hbm.at[lax.rem(place, F // TC)], table.at[1]),
                )
            )
        ]
        load_centres, load_owner, load_azimuth, load_pulses, *load_tables = loads
        for load in loads:
            load.start()

        for step in range(2):
            fields[step, 0:RAD, :] = jnp.full((RAD, TC), OUTSIDE, jnp.float32)
            fields[step, RAD + TR :, :] = jnp.full((RAD, TC), OUTSIDE, jnp.float32)
            lefts[step] = jnp.full((TR, TC), OUTSIDE, jnp.float32)
            rights[step] = jnp.full((TR, TC), OUTSIDE, jnp.float32)
        def beside(step):
            where = place + step
            return {"col": where // n_subs, "sub": where % n_subs}

        has_left = place > 0
        has_right = place < n_tiles - 1
        has_above = row > 0
        has_below = row < n_rows - 1

        barrier = pltpu.get_barrier_semaphore()
        for step in range(1, n_rows):
            pl.semaphore_signal(
                barrier, inc=1, device_id={"row": lax.rem(row + step, n_rows)}, device_id_type=MESH
            )

        @pl.when(has_left)
        def _():
            pl.semaphore_signal(barrier, inc=1, device_id=beside(-1), device_id_type=MESH)

        @pl.when(has_right)
        def _():
            pl.semaphore_signal(barrier, inc=1, device_id=beside(1), device_id_type=MESH)

        load_centres.wait()
        packed = centres[0, 0, 0] * 65536 + centres[0, 0, 1]
        shifts[row] = jnp.full((8, LANES), packed, jnp.int32)

        load_owner.wait()
        load_azimuth.wait()
        which_block = lax.broadcasted_iota(jnp.int32, (1, depth), 1) // (2 * half)
        mine = jnp.zeros((1, depth), jnp.float32)
        for block in range(NBLK):
            held = jnp.where(owner[block] == row, 1.0, 0.0)
            mine = jnp.where(which_block == block, held, mine)
        masked = azimuth[...] * mine.astype(jnp.bfloat16)

        pl.semaphore_wait(
            barrier, n_rows - 1 + has_left.astype(jnp.int32) + has_right.astype(jnp.int32)
        )

        shift_copies = []
        for step in range(1, n_rows):
            copy = pltpu.make_async_remote_copy(
                src_ref=shifts.at[row],
                dst_ref=shifts.at[row],
                send_sem=shift_send.at[step],
                recv_sem=shift_recv.at[step],
                device_id={"row": lax.rem(row + step, n_rows)},
                device_id_type=MESH,
            )
            copy.start()
            shift_copies.append(copy)

        load_pulses.wait()
        focused = jnp.dot(masked, pulses[...], preferred_element_type=jnp.float32)
        focus_out[...] = focused.astype(jnp.bfloat16)
        to_other = pltpu.make_async_remote_copy(
            src_ref=focus_out,
            dst_ref=focus_in,
            send_sem=sub_send,
            recv_sem=sub_recv,
            device_id={"sub": other},
            device_id_type=MESH,
        )
        to_other.start()
        focus[...] = focused
        for load in load_tables:
            load.wait()
        to_other.wait_recv()
        whole = (focus[...] + focus_in[...].astype(jnp.float32)).astype(jnp.bfloat16)
        for side in range(2):
            product = jnp.dot(whole, table[side], preferred_element_type=jnp.float32)
            real = product[:all_rows, :TC] - product[all_rows:, TC:]
            imag = product[:all_rows, TC:] + product[all_rows:, :TC]
            for number, values in enumerate((real, imag)):
                formed[number, side, TR:, :] = values
                formed[number, side, 0:TR, :] = values[all_rows - TR :]

        for copy in shift_copies:
            copy.wait_recv()
        line = lax.broadcasted_iota(jnp.int32, (TR, TC), 1)

        def tile_of(which):
            packed = shifts[which][0, 0]
            down = packed >> 16
            across = packed & 65535
            at = pl.ds((which + 1) * TR - down, TR)
            parts = []
            for number in range(2):
                values = jnp.where(
                    line < TC - across, formed[number, 1, at, :], formed[number, 0, at, :]
                )
                parts.append(pltpu.roll(values, across, 1))
            return parts

        row_copies = []
        for step in range(1, n_rows):
            target = lax.rem(row + step, n_rows)
            for number, values in enumerate(tile_of(target)):
                wire[step, number] = values.astype(jnp.bfloat16)
            copy = pltpu.make_async_remote_copy(
                src_ref=wire.at[step],
                dst_ref=wire_in.at[step],
                send_sem=row_send.at[step],
                recv_sem=row_recv.at[step],
                device_id={"row": target},
                device_id_type=MESH,
            )
            copy.start()
            row_copies.append(copy)
        image = tile_of(row)
        for step, copy in enumerate(row_copies, 1):
            copy.wait_recv()
            image = [image[number] + wire_in[step, number].astype(jnp.float32) for number in range(2)]
        field = (image[0] * image[0] + image[1] * image[1]) * UNIT

        sent = []

        def exchange(step, field):
            fields[step, RAD : RAD + TR, :] = field
            low = fields.at[step, RAD : 2 * RAD]
            high = fields.at[step, TR : RAD + TR]
            whole = fields.at[step, RAD : RAD + TR]
            plans = (
                (has_left, has_right, whole, rights.at[step], beside(-1)),
                (has_right, has_left, whole, lefts.at[step], beside(1)),
                (has_above, has_below, low, fields.at[step, RAD + TR :], {"row": row - 1}),
                (has_below, has_above, high, fields.at[step, 0:RAD], {"row": row + 1}),
            )
            arriving = []
            for number, (sends, receives, source, target, device) in enumerate(plans):
                copy = pltpu.make_async_remote_copy(
                    src_ref=source,
                    dst_ref=target,
                    send_sem=halo_send.at[step, number],
                    recv_sem=halo_recv.at[step, number],
                    device_id=device,
                    device_id_type=MESH,
                )
                sent.append((sends, copy))
                arriving.append((receives, copy))

                @pl.when(sends)
                def _():
                    copy.start()

            return arriving

        def arrive(arriving):
            for receives, copy in arriving:

                @pl.when(receives)
                def _():
                    copy.wait_recv()

        arriving = exchange(0, field)
        packed_ref[0:TR, :] = image[0]
        packed_ref[TR : 2 * TR, :] = image[1]
        first = fields.at[0]
        sums = along_rows(first, begin(first), True)
        arrive(arriving)
        sums = along_rows(first, sums, False)
        outer = jnp.where(line < RAD, rights[0], lefts[0])
        field = ratio(along_cols(first, outer, sums))

        arriving = exchange(1, field)
        to_other.wait_send()
        for copy in shift_copies + row_copies:
            copy.wait_send()
        arrive(arriving)
        packed_ref[2 * TR : 4 * TR, :] = fields[1]
        packed_ref[4 * TR :, :] = jnp.where(line < RAD, rights[1], lefts[1])
        for sends, copy in sent:

            @pl.when(sends)
            def _():
                copy.wait_send()

    dma = pltpu.SemaphoreType.DMA
    vmem = pl.BlockSpec(memory_space=pltpu.VMEM)
    hbm = pl.BlockSpec(memory_space=pltpu.HBM)
    form_call = pl.pallas_call(
        kernel,
        out_shape=jax.ShapeDtypeStruct((5 * TR, TC), jnp.float32),
        in_specs=[hbm] * 5,
        out_specs=vmem,
        scratch_shapes=[
            pltpu.SMEM((NBLK,), jnp.int32),
            pltpu.SMEM((1, 1, 2), jnp.int32),
            pltpu.VMEM((depth, F), jnp.bfloat16),
            pltpu.VMEM((2 * all_rows, depth), jnp.bfloat16),
            pltpu.VMEM((2, F, 2 * TC), jnp.bfloat16),
            pltpu.VMEM((2 * all_rows, F), jnp.float32),
            pltpu.VMEM((2 * all_rows, F), jnp.bfloat16),
            pltpu.VMEM((2 * all_rows, F), jnp.bfloat16),
            pltpu.VMEM((2, 2, TR + all_rows, TC), jnp.float32),
            pltpu.VMEM((n_rows, 8, LANES), jnp.int32),
            pltpu.VMEM((n_rows, 2, TR, TC), jnp.bfloat16),
            pltpu.VMEM((n_rows, 2, TR, TC), jnp.bfloat16),
            pltpu.VMEM((2, TR + 2 * RAD, TC), jnp.float32),
            pltpu.VMEM((2, TR, TC), jnp.float32),
            pltpu.VMEM((2, TR, TC), jnp.float32),
            dma((6,)),
            dma((n_rows,)),
            dma((n_rows,)),
            dma,
            dma,
            dma((n_rows,)),
            dma((n_rows,)),
            dma((2, 4)),
            dma((2, 4)),
        ],
        compiler_params=pltpu.CompilerParams(
            collective_id=0, has_side_effects=True, vmem_limit_bytes=int(53.5 * 2**20)
        ),
        cost_estimate=pl.CostEstimate(
            flops=8 * all_rows * depth * F, bytes_accessed=3 * 2**20, transcendentals=2**20
        ),
    )
    last_call = pl.pallas_call(
        last_pass,
        out_shape=(
            jax.ShapeDtypeStruct((TR, 2, TC), jnp.float32),
            jax.ShapeDtypeStruct((TR, TC), jnp.float32),
        ),
        in_specs=[vmem],
        out_specs=(hbm, hbm),
        scratch_shapes=[
            pltpu.VMEM((TR, 2, TC), jnp.float32),
            pltpu.VMEM((TR, TC), jnp.float32),
            dma((2,)),
        ],
        cost_estimate=pl.CostEstimate(flops=2**20, bytes_accessed=2**17, transcendentals=2**18),
    )
    return form_call, last_call


def solution(mesh):
    n_rows, n_cols, n_subs = (mesh.shape[name] for name in ("row", "col", "sub"))
    form_call, last_call = make_kernel(n_rows, n_cols, n_subs)
    azimuth = azimuth_table(TR * n_rows, n_subs)
    table = range_table()

    def per_device(pulses, owner, centres):
        return last_call(form_call(owner, centres, pulses.reshape(-1, F), azimuth, table))

    return jax.shard_map(
        per_device,
        mesh=mesh,
        in_specs=(
            P(None, ("groups", "row"), None, "sub", None),
            P("groups"),
            P(("groups", "row"), "col", None),
        ),
        out_specs=(
            P(("groups", "row"), None, ("col", "sub")),
            P(("groups", "row"), ("col", "sub")),
        ),
        check_vma=False,
    )
```

```python
import math

import jax
import jax.numpy as jnp
import numpy as np
from jax import lax
from jax.experimental import pallas as pl
from jax.experimental.pallas import tpu as pltpu
from jax.sharding import PartitionSpec as P

F = 1024
PB = 256
NBLK = 2
TR = 32
TC = 128
RAD = 16
LANES = 128

SIGMA_RANGE = 1.0
LOG2E = math.log2(math.e)
OUTSIDE = 1.0e18
UNIT = math.sqrt(0.5 * LOG2E) / SIGMA_RANGE
MESH = pl.DeviceIdType.MESH


def constant(table):
    return jnp.asarray(table.astype(np.float32), jnp.bfloat16)


def range_table():
    index = np.arange(F)[:, None] * np.arange(F)[None, :] % F
    angle = (2.0 * np.pi / F * index).reshape(F, F // TC, TC).transpose(1, 0, 2)
    return constant(np.concatenate([np.cos(angle), -np.sin(angle)], axis=2) / math.sqrt(F))


def azimuth_table(all_rows, n_subs):
    index = np.arange(all_rows)[:, None] * np.arange(NBLK * PB)[None, :] % all_rows
    angle = (2.0 * np.pi / all_rows * index).reshape(all_rows, NBLK, n_subs, PB // n_subs)
    c = np.cos(angle).transpose(2, 0, 1, 3)
    s = np.sin(angle).transpose(2, 0, 1, 3)
    parts = [np.stack([c, s], axis=3), np.stack([-s, c], axis=3)]
    table = np.concatenate([part.reshape(n_subs, all_rows, -1) for part in parts], axis=1)
    return constant(table / math.sqrt(NBLK * PB))


def add(sums, nears, center, distance):
    top = bottom = None
    for near in nears:
        contrast = near - center
        kernel = jnp.exp2(-SPATIAL[distance] - contrast * contrast)
        term = kernel * near
        top = term if top is None else top + term
        bottom = kernel if bottom is None else bottom + kernel
    return (sums[0] + top, sums[1] + bottom) if nears else sums


SPATIAL = [2.0 * d * d / (RAD * RAD) * LOG2E for d in range(RAD + 1)]


def begin(field):
    centers = [field[RAD + first : RAD + first + 8, :] for first in range(0, TR, 8)]
    return [(center, jnp.ones_like(center)) for center in centers]


def along_rows(field, sums, inner):
    sums = list(sums)
    centers = [field[RAD + first : RAD + first + 8, :] for first in range(0, TR, 8)]
    for distance in range(1, RAD + 1):
        for number, first in enumerate(range(0, TR, 8)):
            nears = [
                field[RAD + low : RAD + low + 8, :]
                for low in (first - distance, first + distance)
                if (0 <= low <= TR - 8) == inner
            ]
            sums[number] = add(sums[number], nears, centers[number], distance)
    return sums


def along_cols(field, outer, sums):
    sums = list(sums)
    lane = lax.broadcasted_iota(jnp.int32, (8, TC), 1)
    centers = [field[RAD + first : RAD + first + 8, :] for first in range(0, TR, 8)]
    outers = [outer[first : first + 8, :] for first in range(0, TR, 8)]
    for distance in range(1, RAD + 1):
        for number, (center, outside) in enumerate(zip(centers, outers)):
            after = jnp.where(lane < distance, outside, center)
            before = jnp.where(lane >= TC - distance, outside, center)
            nears = [
                pltpu.roll(after, TC - distance, 1),
                pltpu.roll(before, distance, 1),
            ]
            sums[number] = add(sums[number], nears, center, distance)
    return sums


def ratio(sums):
    return jnp.concatenate([numerator / weight for numerator, weight in sums], axis=0)


def last_pass(packed, image_hbm, despeckled_hbm, image, despeckled, sems):
    image[:, 0, :] = packed[0:TR, :]
    image[:, 1, :] = packed[TR : 2 * TR, :]
    save_image = pltpu.make_async_copy(image, image_hbm, sems.at[0])
    save_image.start()
    field = packed.at[2 * TR : 4 * TR]
    outer = packed[4 * TR : 5 * TR, :]
    sums = along_rows(field, begin(field), True)
    sums = along_rows(field, sums, False)
    sums = along_cols(field, outer, sums)
    despeckled[...] = ratio(sums) * (1.0 / UNIT)
    save = pltpu.make_async_copy(despeckled, despeckled_hbm, sems.at[1])
    save.start()
    save_image.wait()
    save.wait()


def make_kernel(n_rows, n_cols, n_subs):
    all_rows = TR * n_rows
    n_tiles = n_cols * n_subs
    half = PB // n_subs
    depth = NBLK * 2 * half

    def kernel(
        owner_hbm, centres_hbm, pulses_hbm, azimuth_hbm, table_hbm, packed_ref,
        owner, centres, pulses, azimuth, table, formed, shifts, part, part_in, wire, wire_in, fields, lefts, rights,
        load_sem, shift_send, shift_recv, sub_send, sub_recv, row_send, row_recv,
        halo_send, halo_recv,
    ):
        row = lax.axis_index("row")
        col = lax.axis_index("col")
        sub = lax.axis_index("sub")
        place = col * n_subs + sub
        other = 1 - sub

        loads = [
            pltpu.make_async_copy(source, target, load_sem.at[number])
            for number, (source, target) in enumerate(
                (
                    (centres_hbm, centres),
                    (owner_hbm, owner),
                    (azimuth_hbm.at[sub], azimuth),
                    (pulses_hbm, pulses),
                    *(
                        (table_hbm.at[lax.rem(col * n_subs + side + F // TC - 1, F // TC)], table.at[side])
                        for side in range(n_subs + 1)
                    ),
                )
            )
        ]
        load_centres, load_owner, load_azimuth, load_pulses, *load_tables = loads
        for load in loads:
            load.start()

        for step in range(2):
            fields[step, 0:RAD, :] = jnp.full((RAD, TC), OUTSIDE, jnp.float32)
            fields[step, RAD + TR :, :] = jnp.full((RAD, TC), OUTSIDE, jnp.float32)
            lefts[step] = jnp.full((TR, TC), OUTSIDE, jnp.float32)
            rights[step] = jnp.full((TR, TC), OUTSIDE, jnp.float32)
        def beside(step):
            where = place + step
            return {"col": where // n_subs, "sub": where % n_subs}

        has_left = place > 0
        has_right = place < n_tiles - 1
        has_above = row > 0
        has_below = row < n_rows - 1

        barrier = pltpu.get_barrier_semaphore()
        for step in range(1, n_rows):
            pl.semaphore_signal(
                barrier, inc=1, device_id={"row": lax.rem(row + step, n_rows)}, device_id_type=MESH
            )

        @pl.when(has_left)
        def _():
            pl.semaphore_signal(barrier, inc=1, device_id=beside(-1), device_id_type=MESH)

        @pl.when(has_right)
        def _():
            pl.semaphore_signal(barrier, inc=1, device_id=beside(1), device_id_type=MESH)

        load_centres.wait()
        packed = centres[0, 0, 0] * 65536 + centres[0, 0, 1]
        shifts[row] = jnp.full((8, LANES), packed, jnp.int32)

        load_owner.wait()
        load_azimuth.wait()
        which_block = lax.broadcasted_iota(jnp.int32, (1, depth), 1) // (2 * half)
        mine = jnp.zeros((1, depth), jnp.float32)
        for block in range(NBLK):
            held = jnp.where(owner[block] == row, 1.0, 0.0)
            mine = jnp.where(which_block == block, held, mine)
        masked = azimuth[...] * mine.astype(jnp.bfloat16)

        pl.semaphore_wait(
            barrier, n_rows - 1 + has_left.astype(jnp.int32) + has_right.astype(jnp.int32)
        )

        shift_copies = []
        for step in range(1, n_rows):
            copy = pltpu.make_async_remote_copy(
                src_ref=shifts.at[row],
                dst_ref=shifts.at[row],
                send_sem=shift_send.at[step],
                recv_sem=shift_recv.at[step],
                device_id={"row": lax.rem(row + step, n_rows)},
                device_id_type=MESH,
            )
            copy.start()
            shift_copies.append(copy)

        load_pulses.wait()
        whole = jnp.dot(masked, pulses[...], preferred_element_type=jnp.float32).astype(jnp.bfloat16)
        for side, load in enumerate(load_tables):
            load.wait()
            product = jnp.dot(whole, table[side], preferred_element_type=jnp.float32)
            real = product[:all_rows, :TC] - product[all_rows:, TC:]
            imag = product[:all_rows, TC:] + product[all_rows:, :TC]
            for number, values in enumerate((real, imag)):
                formed[number, side, TR:, :] = values
                formed[number, side, 0:TR, :] = values[all_rows - TR :]

        for copy in shift_copies:
            copy.wait_recv()
        line = lax.broadcasted_iota(jnp.int32, (TR, TC), 1)

        def tile_of(which, core):
            packed = shifts[which][0, 0]
            down = packed >> 16
            across = packed & 65535
            at = pl.ds((which + 1) * TR - down, TR)
            parts = []
            for number in range(2):
                values = jnp.where(
                    line < TC - across, formed[number, core + 1, at, :], formed[number, core, at, :]
                )
                parts.append(pltpu.roll(values, across, 1))
            return parts

        for step in range(n_rows):
            which = lax.rem(row + step, n_rows)
            for number, values in enumerate(tile_of(which, other)):
                part[step, number] = values
        to_other = pltpu.make_async_remote_copy(
            src_ref=part,
            dst_ref=part_in,
            send_sem=sub_send,
            recv_sem=sub_recv,
            device_id={"sub": other},
            device_id_type=MESH,
        )
        to_other.start()
        tiles = [tile_of(lax.rem(row + step, n_rows), sub) for step in range(n_rows)]
        to_other.wait_recv()

        row_copies = []
        for step in range(1, n_rows):
            for number in range(2):
                wire[step, number] = (tiles[step][number] + part_in[step, number]).astype(jnp.bfloat16)
            copy = pltpu.make_async_remote_copy(
                src_ref=wire.at[step],
                dst_ref=wire_in.at[step],
                send_sem=row_send.at[step],
                recv_sem=row_recv.at[step],
                device_id={"row": lax.rem(row + step, n_rows)},
                device_id_type=MESH,
            )
            copy.start()
            row_copies.append(copy)
        image = [tiles[0][number] + part_in[0, number] for number in range(2)]
        for step, copy in enumerate(row_copies, 1):
            copy.wait_recv()
            image = [image[number] + wire_in[step, number].astype(jnp.float32) for number in range(2)]
        field = (image[0] * image[0] + image[1] * image[1]) * UNIT

        sent = []

        def exchange(step, field):
            fields[step, RAD : RAD + TR, :] = field
            low = fields.at[step, RAD : 2 * RAD]
            high = fields.at[step, TR : RAD + TR]
            whole = fields.at[step, RAD : RAD + TR]
            plans = (
                (has_left, has_right, whole, rights.at[step], beside(-1)),
                (has_right, has_left, whole, lefts.at[step], beside(1)),
                (has_above, has_below, low, fields.at[step, RAD + TR :], {"row": row - 1}),
                (has_below, has_above, high, fields.at[step, 0:RAD], {"row": row + 1}),
            )
            arriving = []
            for number, (sends, receives, source, target, device) in enumerate(plans):
                copy = pltpu.make_async_remote_copy(
                    src_ref=source,
                    dst_ref=target,
                    send_sem=halo_send.at[step, number],
                    recv_sem=halo_recv.at[step, number],
                    device_id=device,
                    device_id_type=MESH,
                )
                sent.append((sends, copy))
                arriving.append((receives, copy))

                @pl.when(sends)
                def _():
                    copy.start()

            return arriving

        def arrive(arriving):
            for receives, copy in arriving:

                @pl.when(receives)
                def _():
                    copy.wait_recv()

        arriving = exchange(0, field)
        packed_ref[0:TR, :] = image[0]
        packed_ref[TR : 2 * TR, :] = image[1]
        first = fields.at[0]
        sums = along_rows(first, begin(first), True)
        arrive(arriving)
        sums = along_rows(first, sums, False)
        outer = jnp.where(line < RAD, rights[0], lefts[0])
        field = ratio(along_cols(first, outer, sums))

        arriving = exchange(1, field)
        to_other.wait_send()
        for copy in shift_copies + row_copies:
            copy.wait_send()
        arrive(arriving)
        packed_ref[2 * TR : 4 * TR, :] = fields[1]
        packed_ref[4 * TR :, :] = jnp.where(line < RAD, rights[1], lefts[1])
        for sends, copy in sent:

            @pl.when(sends)
            def _():
                copy.wait_send()

    dma = pltpu.SemaphoreType.DMA
    vmem = pl.BlockSpec(memory_space=pltpu.VMEM)
    hbm = pl.BlockSpec(memory_space=pltpu.HBM)
    form_call = pl.pallas_call(
        kernel,
        out_shape=jax.ShapeDtypeStruct((5 * TR, TC), jnp.float32),
        in_specs=[hbm] * 5,
        out_specs=vmem,
        scratch_shapes=[
            pltpu.SMEM((NBLK,), jnp.int32),
            pltpu.SMEM((1, 1, 2), jnp.int32),
            pltpu.VMEM((depth, F), jnp.bfloat16),
            pltpu.VMEM((2 * all_rows, depth), jnp.bfloat16),
            pltpu.VMEM((n_subs + 1, F, 2 * TC), jnp.bfloat16),
            pltpu.VMEM((2, n_subs + 1, TR + all_rows, TC), jnp.float32),
            pltpu.VMEM((n_rows, 8, LANES), jnp.int32),
            pltpu.VMEM((n_rows, 2, TR, TC), jnp.float32),
            pltpu.VMEM((n_rows, 2, TR, TC), jnp.float32),
            pltpu.VMEM((n_rows, 2, TR, TC), jnp.bfloat16),
            pltpu.VMEM((n_rows, 2, TR, TC), jnp.bfloat16),
            pltpu.VMEM((2, TR + 2 * RAD, TC), jnp.float32),
            pltpu.VMEM((2, TR, TC), jnp.float32),
            pltpu.VMEM((2, TR, TC), jnp.float32),
            dma((5 + n_subs,)),
            dma((n_rows,)),
            dma((n_rows,)),
            dma,
            dma,
            dma((n_rows,)),
            dma((n_rows,)),
            dma((2, 4)),
            dma((2, 4)),
        ],
        compiler_params=pltpu.CompilerParams(
            collective_id=0, has_side_effects=True, vmem_limit_bytes=60 * 2**20
        ),
        cost_estimate=pl.CostEstimate(
            flops=8 * all_rows * depth * F, bytes_accessed=3 * 2**20, transcendentals=2**20
        ),
    )
    last_call = pl.pallas_call(
        last_pass,
        out_shape=(
            jax.ShapeDtypeStruct((TR, 2, TC), jnp.float32),
            jax.ShapeDtypeStruct((TR, TC), jnp.float32),
        ),
        in_specs=[vmem],
        out_specs=(hbm, hbm),
        scratch_shapes=[
            pltpu.VMEM((TR, 2, TC), jnp.float32),
            pltpu.VMEM((TR, TC), jnp.float32),
            dma((2,)),
        ],
        cost_estimate=pl.CostEstimate(flops=2**20, bytes_accessed=2**17, transcendentals=2**18),
    )
    return form_call, last_call


def solution(mesh):
    n_rows, n_cols, n_subs = (mesh.shape[name] for name in ("row", "col", "sub"))
    form_call, last_call = make_kernel(n_rows, n_cols, n_subs)
    azimuth = azimuth_table(TR * n_rows, n_subs)
    table = range_table()

    def per_device(pulses, owner, centres):
        return last_call(form_call(owner, centres, pulses.reshape(-1, F), azimuth, table))

    return jax.shard_map(
        per_device,
        mesh=mesh,
        in_specs=(
            P(None, ("groups", "row"), None, "sub", None),
            P("groups"),
            P(("groups", "row"), "col", None),
        ),
        out_specs=(
            P(("groups", "row"), None, ("col", "sub")),
            P(("groups", "row"), ("col", "sub")),
        ),
        check_vma=False,
    )
```

```python
import math

import jax
import jax.numpy as jnp
import numpy as np
from jax import lax
from jax.experimental import pallas as pl
from jax.experimental.pallas import tpu as pltpu
from jax.sharding import PartitionSpec as P

F = 1024
PB = 256
NBLK = 2
TR = 32
TC = 128
RAD = 16
LANES = 128

SIGMA_RANGE = 1.0
LOG2E = math.log2(math.e)
OUTSIDE = 1.0e18
UNIT = math.sqrt(0.5 * LOG2E) / SIGMA_RANGE
MESH = pl.DeviceIdType.MESH


def constant(table):
    return jnp.asarray(table.astype(np.float32), jnp.bfloat16)


def range_table():
    index = np.arange(F)[:, None] * np.arange(F)[None, :] % F
    angle = (2.0 * np.pi / F * index).reshape(F, F // TC, TC).transpose(1, 0, 2)
    return constant(np.concatenate([np.cos(angle), -np.sin(angle)], axis=2) / math.sqrt(F))


def azimuth_table(all_rows, n_subs):
    index = np.arange(all_rows)[:, None] * np.arange(NBLK * PB)[None, :] % all_rows
    angle = (2.0 * np.pi / all_rows * index).reshape(all_rows, NBLK, n_subs, PB // n_subs)
    c = np.cos(angle).transpose(2, 0, 1, 3)
    s = np.sin(angle).transpose(2, 0, 1, 3)
    parts = [np.stack([c, s], axis=3), np.stack([-s, c], axis=3)]
    table = np.concatenate([part.reshape(n_subs, all_rows, -1) for part in parts], axis=1)
    return constant(table / math.sqrt(NBLK * PB))


def add(sums, nears, center, distance):
    top = bottom = None
    for near in nears:
        contrast = near - center
        kernel = jnp.exp2(-SPATIAL[distance] - contrast * contrast)
        term = kernel * near
        top = term if top is None else top + term
        bottom = kernel if bottom is None else bottom + kernel
    return (sums[0] + top, sums[1] + bottom) if nears else sums


SPATIAL = [2.0 * d * d / (RAD * RAD) * LOG2E for d in range(RAD + 1)]


def begin(field):
    centers = [field[RAD + first : RAD + first + 8, :] for first in range(0, TR, 8)]
    return [(center, jnp.ones_like(center)) for center in centers]


def along_rows(field, sums, inner):
    sums = list(sums)
    centers = [field[RAD + first : RAD + first + 8, :] for first in range(0, TR, 8)]
    for distance in range(1, RAD + 1):
        for number, first in enumerate(range(0, TR, 8)):
            nears = [
                field[RAD + low : RAD + low + 8, :]
                for low in (first - distance, first + distance)
                if (0 <= low <= TR - 8) == inner
            ]
            sums[number] = add(sums[number], nears, centers[number], distance)
    return sums


def along_cols(field, sums):
    sums = list(sums)
    lane = lax.broadcasted_iota(jnp.int32, (8, TC), 1)
    centers = [field[RAD + first : RAD + first + 8, :] for first in range(0, TR, 8)]
    for distance in range(1, RAD + 1):
        for number, center in enumerate(centers):
            after = jnp.where(lane < distance, OUTSIDE, center)
            before = jnp.where(lane >= TC - distance, OUTSIDE, center)
            nears = [
                pltpu.roll(after, TC - distance, 1),
                pltpu.roll(before, distance, 1),
            ]
            sums[number] = add(sums[number], nears, center, distance)
    return sums


def beside_tile(field, outer, sums):
    sums = list(sums)
    lane = lax.broadcasted_iota(jnp.int32, (8, TC), 1)
    centers = [field[RAD + first : RAD + first + 8, :] for first in range(0, TR, 8)]
    outers = [outer[first : first + 8, :] for first in range(0, TR, 8)]
    for distance in range(1, RAD + 1):
        for number, (center, outside) in enumerate(zip(centers, outers)):
            before = pltpu.roll(outside, distance, 1)
            after = pltpu.roll(outside, TC - distance, 1)
            near = jnp.where(lane >= TC - distance, after, OUTSIDE)
            near = jnp.where(lane < distance, before, near)
            sums[number] = add(sums[number], [near], center, distance)
    return sums


def inside_tile(field):
    return along_cols(field, along_rows(field, begin(field), True))


def outside_tile(field, outer, sums):
    return beside_tile(field, outer, along_rows(field, sums, False))


def ratio(sums):
    return jnp.concatenate([numerator / weight for numerator, weight in sums], axis=0)


def last_pass(packed, image_hbm, despeckled_hbm, image, despeckled, sems):
    image[:, 0, :] = packed[0:TR, :]
    image[:, 1, :] = packed[TR : 2 * TR, :]
    save_image = pltpu.make_async_copy(image, image_hbm, sems.at[0])
    save_image.start()
    field = packed.at[2 * TR : 4 * TR]
    outer = packed[4 * TR : 5 * TR, :]
    sums = [
        (packed[first : first + 8, :], packed[TR + first : TR + first + 8, :])
        for first in range(5 * TR, 6 * TR, 8)
    ]
    sums = outside_tile(field, outer, sums)
    despeckled[...] = ratio(sums) * (1.0 / UNIT)
    save = pltpu.make_async_copy(despeckled, despeckled_hbm, sems.at[1])
    save.start()
    save_image.wait()
    save.wait()


def make_kernel(n_rows, n_cols, n_subs):
    all_rows = TR * n_rows
    n_tiles = n_cols * n_subs
    half = PB // n_subs
    depth = NBLK * 2 * half

    def kernel(
        owner_hbm, centres_hbm, pulses_hbm, azimuth_hbm, table_hbm, packed_ref,
        owner, centres, pulses, azimuth, table, formed, shifts, part, part_in, wire, wire_in, fields, lefts, rights,
        load_sem, shift_send, shift_recv, sub_send, sub_recv, row_send, row_recv,
        halo_send, halo_recv,
    ):
        row = lax.axis_index("row")
        col = lax.axis_index("col")
        sub = lax.axis_index("sub")
        place = col * n_subs + sub
        other = 1 - sub

        loads = [
            pltpu.make_async_copy(source, target, load_sem.at[number])
            for number, (source, target) in enumerate(
                (
                    (centres_hbm, centres),
                    (owner_hbm, owner),
                    (azimuth_hbm.at[sub], azimuth),
                    (pulses_hbm, pulses),
                    *(
                        (table_hbm.at[lax.rem(col * n_subs + side + F // TC - 1, F // TC)], table.at[side])
                        for side in range(n_subs + 1)
                    ),
                )
            )
        ]
        load_centres, load_owner, load_azimuth, load_pulses, *load_tables = loads
        for load in loads:
            load.start()

        for step in range(2):
            fields[step, 0:RAD, :] = jnp.full((RAD, TC), OUTSIDE, jnp.float32)
            fields[step, RAD + TR :, :] = jnp.full((RAD, TC), OUTSIDE, jnp.float32)
            lefts[step] = jnp.full((TR, TC), OUTSIDE, jnp.float32)
            rights[step] = jnp.full((TR, TC), OUTSIDE, jnp.float32)
        def beside(step):
            where = place + step
            return {"col": where // n_subs, "sub": where % n_subs}

        has_left = place > 0
        has_right = place < n_tiles - 1
        has_above = row > 0
        has_below = row < n_rows - 1

        barrier = pltpu.get_barrier_semaphore()
        for step in range(1, n_rows):
            pl.semaphore_signal(
                barrier, inc=1, device_id={"row": lax.rem(row + step, n_rows)}, device_id_type=MESH
            )

        @pl.when(has_left)
        def _():
            pl.semaphore_signal(barrier, inc=1, device_id=beside(-1), device_id_type=MESH)

        @pl.when(has_right)
        def _():
            pl.semaphore_signal(barrier, inc=1, device_id=beside(1), device_id_type=MESH)

        load_centres.wait()
        packed = centres[0, 0, 0] * 65536 + centres[0, 0, 1]
        shifts[row] = jnp.full((8, LANES), packed, jnp.int32)

        load_owner.wait()
        load_azimuth.wait()
        which_block = lax.broadcasted_iota(jnp.int32, (1, depth), 1) // (2 * half)
        mine = jnp.zeros((1, depth), jnp.float32)
        for block in range(NBLK):
            held = jnp.where(owner[block] == row, 1.0, 0.0)
            mine = jnp.where(which_block == block, held, mine)
        masked = azimuth[...] * mine.astype(jnp.bfloat16)

        pl.semaphore_wait(
            barrier, n_rows - 1 + has_left.astype(jnp.int32) + has_right.astype(jnp.int32)
        )

        shift_copies = []
        for step in range(1, n_rows):
            copy = pltpu.make_async_remote_copy(
                src_ref=shifts.at[row],
                dst_ref=shifts.at[row],
                send_sem=shift_send.at[step],
                recv_sem=shift_recv.at[step],
                device_id={"row": lax.rem(row + step, n_rows)},
                device_id_type=MESH,
            )
            copy.start()
            shift_copies.append(copy)

        load_pulses.wait()
        whole = jnp.dot(masked, pulses[...], preferred_element_type=jnp.float32).astype(jnp.bfloat16)
        for side, load in enumerate(load_tables):
            load.wait()
            product = jnp.dot(whole, table[side], preferred_element_type=jnp.float32)
            real = product[:all_rows, :TC] - product[all_rows:, TC:]
            imag = product[:all_rows, TC:] + product[all_rows:, :TC]
            for number, values in enumerate((real, imag)):
                formed[number, side, TR:, :] = values
                formed[number, side, 0:TR, :] = values[all_rows - TR :]

        for copy in shift_copies:
            copy.wait_recv()
        line = lax.broadcasted_iota(jnp.int32, (TR, TC), 1)

        def tile_of(which, core):
            packed = shifts[which][0, 0]
            down = packed >> 16
            across = packed & 65535
            at = pl.ds((which + 1) * TR - down, TR)
            parts = []
            for number in range(2):
                values = jnp.where(
                    line < TC - across, formed[number, core + 1, at, :], formed[number, core, at, :]
                )
                parts.append(pltpu.roll(values, across, 1))
            return parts

        for step in range(n_rows):
            which = lax.rem(row + step, n_rows)
            for number, values in enumerate(tile_of(which, other)):
                part[step, number] = values
        to_other = pltpu.make_async_remote_copy(
            src_ref=part,
            dst_ref=part_in,
            send_sem=sub_send,
            recv_sem=sub_recv,
            device_id={"sub": other},
            device_id_type=MESH,
        )
        to_other.start()
        tiles = [tile_of(lax.rem(row + step, n_rows), sub) for step in range(n_rows)]
        to_other.wait_recv()

        row_copies = []
        for step in range(1, n_rows):
            for number in range(2):
                wire[step, number] = (tiles[step][number] + part_in[step, number]).astype(jnp.bfloat16)
            copy = pltpu.make_async_remote_copy(
                src_ref=wire.at[step],
                dst_ref=wire_in.at[step],
                send_sem=row_send.at[step],
                recv_sem=row_recv.at[step],
                device_id={"row": lax.rem(row + step, n_rows)},
                device_id_type=MESH,
            )
            copy.start()
            row_copies.append(copy)
        image = [tiles[0][number] + part_in[0, number] for number in range(2)]
        for step, copy in enumerate(row_copies, 1):
            copy.wait_recv()
            image = [image[number] + wire_in[step, number].astype(jnp.float32) for number in range(2)]
        field = (image[0] * image[0] + image[1] * image[1]) * UNIT

        sent = []

        def exchange(step, field):
            fields[step, RAD : RAD + TR, :] = field
            low = fields.at[step, RAD : 2 * RAD]
            high = fields.at[step, TR : RAD + TR]
            whole = fields.at[step, RAD : RAD + TR]
            plans = (
                (has_left, has_right, whole, rights.at[step], beside(-1)),
                (has_right, has_left, whole, lefts.at[step], beside(1)),
                (has_above, has_below, low, fields.at[step, RAD + TR :], {"row": row - 1}),
                (has_below, has_above, high, fields.at[step, 0:RAD], {"row": row + 1}),
            )
            arriving = []
            for number, (sends, receives, source, target, device) in enumerate(plans):
                copy = pltpu.make_async_remote_copy(
                    src_ref=source,
                    dst_ref=target,
                    send_sem=halo_send.at[step, number],
                    recv_sem=halo_recv.at[step, number],
                    device_id=device,
                    device_id_type=MESH,
                )
                sent.append((sends, copy))
                arriving.append((receives, copy))

                @pl.when(sends)
                def _():
                    copy.start()

            return arriving

        def arrive(arriving):
            for receives, copy in arriving:

                @pl.when(receives)
                def _():
                    copy.wait_recv()

        arriving = exchange(0, field)
        packed_ref[0:TR, :] = image[0]
        packed_ref[TR : 2 * TR, :] = image[1]
        first = fields.at[0]
        sums = inside_tile(first)
        arrive(arriving)
        outer = jnp.where(line < RAD, rights[0], lefts[0])
        field = ratio(outside_tile(first, outer, sums))

        arriving = exchange(1, field)
        for number, (top, bottom) in enumerate(inside_tile(fields.at[1])):
            packed_ref[5 * TR + 8 * number : 5 * TR + 8 * number + 8, :] = top
            packed_ref[6 * TR + 8 * number : 6 * TR + 8 * number + 8, :] = bottom
        to_other.wait_send()
        for copy in shift_copies + row_copies:
            copy.wait_send()
        arrive(arriving)
        packed_ref[2 * TR : 4 * TR, :] = fields[1]
        packed_ref[4 * TR : 5 * TR, :] = jnp.where(line < RAD, rights[1], lefts[1])
        for sends, copy in sent:

            @pl.when(sends)
            def _():
                copy.wait_send()

    dma = pltpu.SemaphoreType.DMA
    vmem = pl.BlockSpec(memory_space=pltpu.VMEM)
    hbm = pl.BlockSpec(memory_space=pltpu.HBM)
    form_call = pl.pallas_call(
        kernel,
        out_shape=jax.ShapeDtypeStruct((7 * TR, TC), jnp.float32),
        in_specs=[hbm] * 5,
        out_specs=vmem,
        scratch_shapes=[
            pltpu.SMEM((NBLK,), jnp.int32),
            pltpu.SMEM((1, 1, 2), jnp.int32),
            pltpu.VMEM((depth, F), jnp.bfloat16),
            pltpu.VMEM((2 * all_rows, depth), jnp.bfloat16),
            pltpu.VMEM((n_subs + 1, F, 2 * TC), jnp.bfloat16),
            pltpu.VMEM((2, n_subs + 1, TR + all_rows, TC), jnp.float32),
            pltpu.VMEM((n_rows, 8, LANES), jnp.int32),
            pltpu.VMEM((n_rows, 2, TR, TC), jnp.float32),
            pltpu.VMEM((n_rows, 2, TR, TC), jnp.float32),
            pltpu.VMEM((n_rows, 2, TR, TC), jnp.bfloat16),
            pltpu.VMEM((n_rows, 2, TR, TC), jnp.bfloat16),
            pltpu.VMEM((2, TR + 2 * RAD, TC), jnp.float32),
            pltpu.VMEM((2, TR, TC), jnp.float32),
            pltpu.VMEM((2, TR, TC), jnp.float32),
            dma((5 + n_subs,)),
            dma((n_rows,)),
            dma((n_rows,)),
            dma,
            dma,
            dma((n_rows,)),
            dma((n_rows,)),
            dma((2, 4)),
            dma((2, 4)),
        ],
        compiler_params=pltpu.CompilerParams(
            collective_id=0, has_side_effects=True, vmem_limit_bytes=60 * 2**20
        ),
        cost_estimate=pl.CostEstimate(
            flops=8 * all_rows * depth * F, bytes_accessed=3 * 2**20, transcendentals=2**20
        ),
    )
    last_call = pl.pallas_call(
        last_pass,
        out_shape=(
            jax.ShapeDtypeStruct((TR, 2, TC), jnp.float32),
            jax.ShapeDtypeStruct((TR, TC), jnp.float32),
        ),
        in_specs=[vmem],
        out_specs=(hbm, hbm),
        scratch_shapes=[
            pltpu.VMEM((TR, 2, TC), jnp.float32),
            pltpu.VMEM((TR, TC), jnp.float32),
            dma((2,)),
        ],
        cost_estimate=pl.CostEstimate(flops=2**20, bytes_accessed=2**17, transcendentals=2**18),
    )
    return form_call, last_call


def solution(mesh):
    n_rows, n_cols, n_subs = (mesh.shape[name] for name in ("row", "col", "sub"))
    form_call, last_call = make_kernel(n_rows, n_cols, n_subs)
    azimuth = azimuth_table(TR * n_rows, n_subs)
    table = range_table()

    def per_device(pulses, owner, centres):
        return last_call(form_call(owner, centres, pulses.reshape(-1, F), azimuth, table))

    return jax.shard_map(
        per_device,
        mesh=mesh,
        in_specs=(
            P(None, ("groups", "row"), None, "sub", None),
            P("groups"),
            P(("groups", "row"), "col", None),
        ),
        out_specs=(
            P(("groups", "row"), None, ("col", "sub")),
            P(("groups", "row"), ("col", "sub")),
        ),
        check_vma=False,
    )
```
